32 devices in a mesh: parts: 2 (over y), wide: 4 (over z), narrow: 4 (over x, core).
Axes of the slice: x: 2, y: 2, z: 4, core: 2. Of those that a mesh axis runs over, the one named last changes fastest.
Arguments:
- recording: bfloat16 [64, 512, 2048], P(('parts', 'wide'), None, 'narrow'), parts along dimension 0, may hold values from -6 to 6
- offsets: int32 [2, 64], P(None, 'parts'), parts along dimension 1, may hold values from -4 to 4
- center_rows: int32 [8, 4, 32], P(('parts', 'wide'), 'narrow'), parts along dimension 0, may hold values from 0 to 127
- center_cols: int32 [8, 4, 32], P(('parts', 'wide'), 'narrow'), parts along dimension 0, may hold values from 0 to 511
- decays: float32 [8, 4, 32], P(('parts', 'wide'), 'narrow'), parts along dimension 0, may hold values from 0.3 to 0.95
Outputs:
- footprints: bfloat16 [8, 4, 32, 135168], P(('parts', 'wide'), 'narrow'), parts along dimension 0
- traces: float32 [8, 4, 32, 16], P(('parts', 'wide'), 'narrow'), parts along dimension 0
- spikes: float32 [8, 4, 32, 16], P(('parts', 'wide'), 'narrow'), parts along dimension 0
The draws below stay inside these ranges and needn't reach their ends.
There are 2 independent parts, one for each index of `parts`. The reference program is written for one: setup_inputs(seed, part) draws one part's arguments, and reference() takes and returns one part's arrays. A program takes and returns all parts, laid end to end along the dimension named above; each array names one. Nothing has to cross between parts.
All inputs are finite; a program needn't handle non-finite values.
Results may differ from the reference program's by a relative error of at most 0.013.
The reference program's roundings to bfloat16 on the way (of `registered`, `observed` and `residual`) count: a program that leaves them out, or rounds other values in their place, can miss the bound.
Values may be sent and summed in bfloat16 or wider, within the bound.
A program may use at most 128 MiB of HBM per device.

```python
import math
import jax
import jax.numpy as jnp
from jax import lax

W = 2048
H = 512
PLANES = 2
VOLUMES = 16
K = 32
MARGIN = 8
SHIFT_MAX = 4
RADIUS = 12
ITERS = 3
FRAMES = 32
PATCH_ROWS = 4
PATCH_COLS = 4
ROWS_PATCH = 128
COLS_PATCH = 512


def place_ends(array, rng, least, largest):
    extent = array.shape
    place = [jax.random.randint(jax.random.fold_in(rng, axis), (), 0, extent[axis]) for axis in range(len(extent))]
    array = array.at[tuple(place)].set(least)
    longest = extent.index(max(extent))
    place[longest] = (place[longest] + 1) % extent[longest]
    return array.at[tuple(place)].set(largest)


def block_scale(own_key, extent, cuts, low, top_value):
    factor_of, own = 1.0, jax.random.fold_in(own_key, 6)
    for axis_at, shards_of in cuts:
        heights = jnp.exp(jax.random.uniform(jax.random.fold_in(own, axis_at), (shards_of,), jnp.float32, low / len(cuts), top_value / len(cuts)))
        factor_of = factor_of * jnp.repeat(heights, extent[axis_at] // shards_of).reshape([-1 if axis == axis_at else 1 for axis in range(len(extent))])
    return factor_of


def bell_draw(key, shape, scale, bound, cuts=(), held_as=jnp.bfloat16):
    gain = block_scale(key, shape, cuts, -0.22, 0.18) if cuts else 1.0
    values = jax.random.normal(key, shape, jnp.float32) * scale * gain
    return jnp.minimum(jnp.maximum(values, -bound), bound).astype(held_as)


def setup_inputs(seed: int = 0, part: int = 0) -> dict:
    streams_of = jax.random.split(jax.random.key(seed), 6)
    part_keys = jax.random.split(jax.random.fold_in(streams_of[5], part), 6)
    recording = bell_draw(part_keys[0], (FRAMES, H, W), 1.0, 6.0, ((0, 4), (2, 4)))
    offsets = place_ends(jax.random.randint(part_keys[1], (2, FRAMES), 0 - SHIFT_MAX, SHIFT_MAX + 1), jax.random.fold_in(part_keys[1], 1), 0 - SHIFT_MAX, SHIFT_MAX).astype(jnp.int32)
    center_rows = place_ends(jax.random.randint(part_keys[2], (PATCH_ROWS, PATCH_COLS, K), 0, ROWS_PATCH), jax.random.fold_in(part_keys[2], 1), 0, ROWS_PATCH - 1).astype(jnp.int32)
    center_cols = place_ends(jax.random.randint(part_keys[3], (PATCH_ROWS, PATCH_COLS, K), 0, COLS_PATCH), jax.random.fold_in(part_keys[3], 1), 0, COLS_PATCH - 1).astype(jnp.int32)
    decays = jnp.clip(jnp.exp(math.log(0.95) - 1.1526795 * jax.random.uniform(part_keys[4], (PATCH_ROWS, PATCH_COLS, K), jnp.float32) ** block_scale(part_keys[4], (PATCH_ROWS, PATCH_COLS, K), ((0, 4), (1, 4)), -0.2, 0.2)), 0.3, 0.95)
    return dict(recording=recording, offsets=offsets, center_rows=center_rows, center_cols=center_cols, decays=decays)


RIDGE = 1.0


def narrowed(values):
    return lax.optimization_barrier(values.astype(jnp.bfloat16)).astype(jnp.float32)


def initial_state(rows_center, cols_center, column_index, rows_patch, cols_patch, width_total):
    ext_width = cols_patch + 2 * MARGIN
    row_pos = jnp.arange(rows_patch, dtype=jnp.int32).astype(jnp.float32)
    col_pos = jnp.arange(ext_width, dtype=jnp.int32) - MARGIN
    global_col = column_index * cols_patch + col_pos
    inside = ((global_col >= 0) & (global_col < width_total)).astype(jnp.float32)
    row_bump = jnp.maximum(0.0, 1.0 - jnp.abs(row_pos[None, :] - rows_center[:, None].astype(jnp.float32)) / RADIUS)
    col_bump = jnp.maximum(0.0, 1.0 - jnp.abs(col_pos.astype(jnp.float32)[None, :] - cols_center[:, None].astype(jnp.float32)) / RADIUS)
    col_bump = col_bump * inside[None, :]
    planar = row_bump[:, :, None] * col_bump[:, None, :]
    initial = jnp.broadcast_to(planar[:, None], (rows_center.shape[0], PLANES, rows_patch, ext_width)).reshape(rows_center.shape[0], -1)
    support = jnp.broadcast_to(inside, (PLANES, rows_patch, ext_width)).reshape(-1)
    return initial, support


def reference(recording, offsets, center_rows, center_cols, decays):
    frames_all, height, width_total = recording.shape
    registered = lax.map(lambda record: jnp.roll(record[0], (record[1], record[2]), (0, 1)), (recording, offsets[0], offsets[1]))
    template = jnp.sum(registered.reshape(PLANES, VOLUMES, height, width_total), axis=1, dtype=jnp.float32) / VOLUMES
    rows_patch = height // PATCH_ROWS
    cols_patch = width_total // PATCH_COLS
    ext_width = cols_patch + 2 * MARGIN

    def one_row(row_index):
        picked = lax.dynamic_slice_in_dim(registered, row_index * rows_patch, rows_patch, 1)
        baseline = lax.dynamic_slice_in_dim(template, row_index * rows_patch, rows_patch, 1)
        observed = (picked.reshape(PLANES, VOLUMES, rows_patch, width_total).astype(jnp.float32) - baseline[:, None]).transpose(1, 0, 2, 3)
        observed = narrowed(observed)
        rows_center = lax.dynamic_index_in_dim(center_rows, row_index, 0, keepdims=False)
        cols_center = lax.dynamic_index_in_dim(center_cols, row_index, 0, keepdims=False)
        decay_row = lax.dynamic_index_in_dim(decays, row_index, 0, keepdims=False)
        pairs = [initial_state(rows_center[column], cols_center[column], column, rows_patch, cols_patch, width_total) for column in range(PATCH_COLS)]
        footprints = jnp.stack([pair[0] for pair in pairs])
        support = jnp.stack([pair[1] for pair in pairs])
        traces = jnp.zeros((PATCH_COLS, K, VOLUMES), jnp.float32)

        def residual_ext(footprints, traces):
            model_ext = jnp.einsum('ckv,cke->cve', narrowed(traces), narrowed(footprints), precision=lax.Precision.HIGHEST)
            model_ext = model_ext.reshape(PATCH_COLS, VOLUMES, PLANES, rows_patch, ext_width)
            canvas = jnp.zeros((VOLUMES, PLANES, rows_patch, width_total + 2 * MARGIN), jnp.float32)
            for column in range(PATCH_COLS):
                canvas = canvas.at[..., column * cols_patch:column * cols_patch + ext_width].add(model_ext[column])
            model_core = canvas[..., MARGIN:MARGIN + width_total]
            residual = narrowed(observed - model_core)
            padded = jnp.pad(residual, ((0, 0), (0, 0), (0, 0), (MARGIN, MARGIN)))
            pieces = [padded[..., column * cols_patch:column * cols_patch + ext_width] for column in range(PATCH_COLS)]
            return jnp.stack(pieces).reshape(PATCH_COLS, VOLUMES, -1)

        for sweep in range(ITERS):
            residual = residual_ext(footprints, traces)
            project = jnp.einsum('cke,cve->ckv', narrowed(footprints), residual, precision=lax.Precision.HIGHEST)
            traces = jnp.maximum(0.0, traces + project / (jnp.sum(footprints * footprints, axis=-1) + RIDGE)[..., None])
            residual = residual_ext(footprints, traces)
            update = jnp.einsum('ckv,cve->cke', narrowed(traces), residual, precision=lax.Precision.HIGHEST)
            footprints = jnp.maximum(0.0, footprints + support[:, None, :] * update / (jnp.sum(traces * traces, axis=-1) + RIDGE)[..., None])
        previous = jnp.concatenate([jnp.zeros((PATCH_COLS, K, 1), jnp.float32), traces[..., :-1]], axis=-1)
        spikes = jnp.maximum(0.0, traces - decay_row[..., None] * previous)
        return footprints.astype(jnp.bfloat16), traces, spikes

    return lax.map(one_row, jnp.arange(PATCH_ROWS, dtype=jnp.int32))
```

```python
import functools

import jax
import jax.numpy as jnp
import numpy as np
from jax import lax
from jax.experimental import pallas as pl
from jax.experimental.pallas import tpu as pltpu
from jax.sharding import PartitionSpec as P

PLANES = 2
VOLUMES = 16
MARGIN = 8
SHIFT_MAX = 4
RADIUS = 12
ITERS = 3
RIDGE = 1.0
EDGE = 2 * MARGIN
LANES = 128
GROUP = 8
VMEM_LIMIT = 48 * 1024 * 1024

f32 = jnp.float32
bf16 = jnp.bfloat16


def roll_lanes(x, shift):
    shift = shift % x.shape[-1]
    return pltpu.roll(x, shift, 1) if shift else x


def lane_iota(shape):
    return lax.broadcasted_iota(jnp.int32, shape, len(shape) - 1)


def pack_kernel(first_ref, last_ref, head_ref, tail_ref):
    frames, height, _ = first_ref.shape
    lane = lane_iota((height, LANES))
    head = jnp.zeros((height, LANES), f32)
    tail = jnp.zeros((height, LANES), f32)
    for f in range(frames):
        here = (lane >= f * EDGE) & (lane < (f + 1) * EDGE)
        head = jnp.where(here, roll_lanes(first_ref[f].astype(f32), f * EDGE), head)
        tail = jnp.where(here, roll_lanes(last_ref[f].astype(f32), (f + 1) * EDGE), tail)
    head_ref[...] = head.astype(bf16)
    tail_ref[...] = tail.astype(bf16)


def pack_edges(recording):
    frames, height, cols = recording.shape
    out = jax.ShapeDtypeStruct((height, LANES), bf16)
    rows = min(height, 128)
    return pl.pallas_call(
        pack_kernel,
        grid=(height // rows,),
        in_specs=[
            pl.BlockSpec((frames, rows, LANES), lambda i: (0, i, 0)),
            pl.BlockSpec((frames, rows, LANES), lambda i: (0, i, cols // LANES - 1)),
        ],
        out_specs=[pl.BlockSpec((rows, LANES), lambda i: (i, 0))] * 2,
        out_shape=[out, out],
        name="pack_edges",
    )(recording, recording)


def register_kernel(shifts_ref, frame_ref, head_ref, tail_ref, core_ref, border_ref, acc_ref):
    f = pl.program_id(0)
    wide, _, rows_patch, cols = core_ref.shape
    height = wide * rows_patch
    width = cols + LANES
    lane = lane_iota((height, LANES))
    back = lax.rem(LANES - f * EDGE, LANES)
    head = pltpu.roll(head_ref[...].astype(f32), back, 1)
    tail = pltpu.roll(tail_ref[...].astype(f32), lax.rem(back + LANES - EDGE, LANES), 1)
    edge = jnp.where(lane < LANES // 2, head, tail)
    frame = jnp.concatenate([frame_ref[0].astype(f32), edge], axis=1)
    row_move = lax.rem(shifts_ref[0, f] + height, height)
    col_move = lax.rem(shifts_ref[1, f] + width, width)
    frame = pltpu.roll(frame, row_move, 0)
    frame = pltpu.roll(frame, col_move, 1)
    core_ref[...] = frame[:, :cols].astype(bf16).reshape(wide, 1, rows_patch, cols)
    moved = pltpu.roll(frame[:, cols:], lax.rem(f * EDGE + MARGIN, LANES), 1)
    here = (lane >= f * EDGE) & (lane < (f + 1) * EDGE)

    @pl.when(f == 0)
    def _():
        acc_ref[...] = jnp.zeros_like(acc_ref)

    acc_ref[...] = jnp.where(here, moved, acc_ref[...])

    @pl.when(f == pl.num_programs(0) - 1)
    def _():
        border_ref[...] = acc_ref[...].astype(bf16).reshape(border_ref.shape)


def register(shifts, recording, head, tail, wide):
    frames, height, cols = recording.shape
    rows_patch = height // wide
    whole = pl.BlockSpec((height, LANES), lambda f: (0, 0))
    return pl.pallas_call(
        register_kernel,
        grid=(frames,),
        in_specs=[
            pl.BlockSpec(memory_space=pltpu.SMEM),
            pl.BlockSpec((1, height, cols), lambda f: (f, 0, 0)),
            whole,
            whole,
        ],
        out_specs=[
            pl.BlockSpec((wide, 1, rows_patch, cols), lambda f: (0, f, 0, 0)),
            pl.BlockSpec((wide, rows_patch, LANES), lambda f: (0, 0, 0)),
        ],
        out_shape=[
            jax.ShapeDtypeStruct((wide, frames, rows_patch, cols), bf16),
            jax.ShapeDtypeStruct((wide, rows_patch, LANES), bf16),
        ],
        scratch_shapes=[pltpu.VMEM((height, LANES), f32)],
        compiler_params=pltpu.CompilerParams(vmem_limit_bytes=VMEM_LIMIT),
        name="register",
    )(shifts, recording, head, tail)


def bump(position, center):
    return jnp.maximum(0.0, 1.0 - jnp.abs(position - center) * (1.0 / RADIUS))


def lane_pieces(cols):
    return [(j * cols, cols if j < GROUP else LANES) for j in range(GROUP + 1)]


NT = (((1,), (1,)), ((), ()))


def nt_dot(a, b):
    return lax.dot_general(a, b, NT, preferred_element_type=f32)


def observe_kernel(
    mix_ref, recv_ref, border_ref, pattern_ref, centers_ref, obs_ref, traces_ref, proj_ref, energy_ref
):
    volumes, rows, cols = recv_ref.shape
    sources = border_ref.shape[0]
    per_source = volumes // sources
    step = pl.program_id(0) * pl.num_programs(1) + pl.program_id(1)
    last = pl.num_programs(0) * pl.num_programs(1) - 1
    base = (pl.program_id(1) * rows).astype(f32)
    mix = mix_ref[...]

    @pl.when(step == 0)
    def _():
        proj_ref[...] = jnp.zeros_like(proj_ref)
        energy_ref[...] = jnp.zeros_like(energy_ref)

    core = jnp.dot(mix, recv_ref[...].reshape(volumes * rows, cols), preferred_element_type=f32)
    strips = [border_ref[s].astype(f32) for s in range(sources)]
    border = jnp.concatenate(
        [
            roll_lanes(strips[v // per_source], -(v % per_source) * EDGE - MARGIN)
            for v in range(volumes)
        ],
        axis=0,
    ).astype(bf16)
    border = jnp.dot(mix, border, preferred_element_type=f32)
    lane = lane_iota((volumes, LANES))
    center_row = centers_ref[:, 0:1]
    center_col = centers_ref[:, 1:2]
    size = GROUP * (cols + EDGE)
    proj = proj_ref[...]
    energy = energy_ref[...]
    for g in range(rows // GROUP):
        carry = None
        for j, (start, width) in enumerate(lane_pieces(cols)):
            if j < GROUP:
                at = (g * GROUP + j) * volumes
                line = jnp.concatenate(
                    [core[at : at + volumes], border[at : at + volumes]], axis=1
                )
                line = roll_lanes(line, MARGIN + EDGE * j)
                first = line[:, :LANES]
                if carry is not None:
                    first = jnp.where(lane < EDGE * j, carry, first)
                carry = line[:, cols:]
                piece = jnp.concatenate([first, line[:, LANES:cols]], axis=1)
            else:
                piece = carry
            low = piece.astype(bf16)
            obs_ref[:, g * size + start : g * size + start + width] = low
            row = pattern_ref[0:1, start : start + width] + (base + g * GROUP)
            col = pattern_ref[1:2, start : start + width]
            inside = pattern_ref[2:3, start : start + width]
            foot = bump(row, center_row) * (bump(col, center_col) * inside)
            proj = proj + nt_dot(foot.astype(bf16), low)
            square = foot * foot
            for c in range(width // LANES):
                energy = energy + square[:, c * LANES : (c + 1) * LANES]
    proj_ref[...] = proj
    energy_ref[...] = energy

    @pl.when(step == last)
    def _():
        total = jnp.sum(energy, axis=1, keepdims=True) + RIDGE
        traces_ref[...] = jnp.maximum(0.0, proj / total)


def observe(received, border, pattern, centers, frames):
    _, rows_patch, cols = received.shape
    comps = centers.shape[0]
    rows = 16
    blocks = rows_patch // rows
    sources = border.shape[0] // PLANES
    size = GROUP * (cols + EDGE)
    same = np.eye(rows)
    mix = np.einsum("yx,vu->yvux", same, np.eye(VOLUMES) - 1.0 / VOLUMES)
    mix = jnp.asarray(mix.reshape(rows * VOLUMES, VOLUMES * rows), bf16)
    flat = PLANES * rows_patch * (cols + EDGE)
    return pl.pallas_call(
        observe_kernel,
        grid=(PLANES, blocks),
        in_specs=[
            pl.BlockSpec(mix.shape, lambda p, y: (0, 0)),
            pl.BlockSpec((VOLUMES, rows, cols), lambda p, y: (p, y, 0)),
            pl.BlockSpec((sources, rows, LANES), lambda p, y: (p, y, 0)),
            pl.BlockSpec((8, size), lambda p, y: (0, 0)),
            pl.BlockSpec((comps, LANES), lambda p, y: (0, 0)),
        ],
        out_specs=[
            pl.BlockSpec((VOLUMES, rows * (cols + EDGE)), lambda p, y: (0, p * blocks + y)),
            pl.BlockSpec((comps, VOLUMES), lambda p, y: (0, 0)),
        ],
        out_shape=[
            jax.ShapeDtypeStruct((VOLUMES, flat), bf16),
            jax.ShapeDtypeStruct((comps, VOLUMES), f32),
        ],
        scratch_shapes=[pltpu.VMEM((comps, VOLUMES), f32), pltpu.VMEM((comps, LANES), f32)],
        compiler_params=pltpu.CompilerParams(vmem_limit_bytes=VMEM_LIMIT),
        name="observe",
    )(mix, received, border, pattern, centers)


def sweep_kernel(rows_patch, cols, first, final, *refs):
    traces_ref, left_ref, right_ref, pattern_ref, centers_ref, obs_ref = refs[:6]
    refs = refs[6:]
    if not first:
        foot_ref, side_ref = refs[:2]
        refs = refs[2:]
    if final:
        (low_ref,) = refs
    else:
        new_foot_ref, new_side_ref, new_traces_ref, proj_ref, energy_ref = refs
    size = GROUP * (cols + EDGE)
    side_size = (GROUP + 1) * LANES
    groups = obs_ref.shape[1] // size
    volumes = obs_ref.shape[0]
    comps = traces_ref.shape[0]
    step = pl.program_id(0)

    eye_at = lax.broadcasted_iota(jnp.int32, (volumes, volumes), 0)
    eye = (eye_at == lax.broadcasted_iota(jnp.int32, (volumes, volumes), 1)).astype(f32).astype(bf16)

    def prepared(ref):
        full = ref[...]
        low = full.astype(bf16)
        flipped = nt_dot(eye, low).astype(bf16)
        scale = 1.0 / (jnp.sum(full * full, axis=1, keepdims=True) + RIDGE)
        return low, flipped, scale

    own, own_t, own_scale = prepared(traces_ref)
    left, left_t, left_scale = prepared(left_ref)
    right, right_t, right_scale = prepared(right_ref)

    if not final:

        @pl.when(step == 0)
        def _():
            proj_ref[...] = jnp.zeros_like(proj_ref)
            energy_ref[...] = jnp.zeros_like(energy_ref)

    def one_group(g, _):
        at = pl.multiple_of(g * size, LANES)
        side_at = pl.multiple_of(g * side_size, LANES)
        base = lax.rem((step * groups + g) * GROUP, rows_patch).astype(f32)
        if not final:
            proj = proj_ref[...]
            energy = energy_ref[...]
        for j, (start, width) in enumerate(lane_pieces(cols)):
            where = pl.ds(at + start, width)
            side_where = pl.ds(side_at + j * LANES, LANES)
            inside = pattern_ref[2:3, start : start + width]
            is_left = pattern_ref[3:4, start : start + LANES]
            is_right = pattern_ref[4:5, start : start + LANES]
            obs = obs_ref[:, where].astype(f32)
            if first:
                row = pattern_ref[0:1, start : start + width] + base
                col = pattern_ref[1:2, start : start + width]
                foot = bump(row, centers_ref[:, 0:1]) * (bump(col, centers_ref[:, 1:2]) * inside)
                row, col = row[:, :LANES], col[:, :LANES]
                side = bump(row, centers_ref[:, 2:3]) * (
                    bump(col + cols, centers_ref[:, 3:4]) * is_left
                ) + bump(row, centers_ref[:, 4:5]) * (
                    bump(col - cols, centers_ref[:, 5:6]) * is_right
                )
            else:
                foot = foot_ref[:, where]
                side = side_ref[:, side_where]

            def residual(foot_low, side):
                model = jnp.dot(own_t, foot_low, preferred_element_type=f32)
                extra = jnp.dot(left_t, (side * is_left).astype(bf16), preferred_element_type=f32)
                extra = extra + jnp.dot(
                    right_t, (side * is_right).astype(bf16), preferred_element_type=f32
                )
                head = model[:, :LANES] + extra
                model = head if width == LANES else jnp.concatenate([head, model[:, LANES:]], axis=1)
                return (obs - model).astype(bf16)

            rest = residual(foot.astype(bf16), side)
            update = jnp.dot(own, rest, preferred_element_type=f32)
            foot = jnp.maximum(0.0, foot + inside * (update * own_scale))
            foot_low = foot.astype(bf16)
            if final:
                low_ref[:, where] = foot_low
                continue
            update_left = jnp.dot(left, rest[:, :LANES], preferred_element_type=f32)
            update_right = jnp.dot(right, rest[:, :LANES], preferred_element_type=f32)
            side = jnp.maximum(
                0.0,
                side
                + is_left * (update_left * left_scale)
                + is_right * (update_right * right_scale),
            )
            new_foot_ref[:, where] = foot
            new_side_ref[:, side_where] = side
            proj = proj + nt_dot(foot_low, residual(foot_low, side))
            square = foot * foot
            for c in range(width // LANES):
                energy = energy + square[:, c * LANES : (c + 1) * LANES]
        if not final:
            proj_ref[...] = proj
            energy_ref[...] = energy
        return 0

    lax.fori_loop(0, groups, one_group, 0)

    if not final:

        @pl.when(step == pl.num_programs(0) - 1)
        def _():
            total = jnp.sum(energy_ref[...], axis=1, keepdims=True) + RIDGE
            new_traces_ref[...] = jnp.maximum(0.0, traces_ref[...] + proj_ref[...] / total)


def sweep(traces, left, right, pattern, centers, observed, state, rows_patch, cols, final):
    comps, volumes = traces.shape
    flat = observed.shape[1]
    groups_all = flat // (GROUP * (cols + EDGE))
    per_block = 4
    blocks = groups_all // per_block
    size = per_block * GROUP * (cols + EDGE)
    side_size = per_block * (GROUP + 1) * LANES
    small = pl.BlockSpec((comps, volumes), lambda i: (0, 0))
    foot_spec = pl.BlockSpec((comps, size), lambda i: (0, i))
    side_spec = pl.BlockSpec((comps, side_size), lambda i: (0, i))
    first = state is None
    in_specs = [
        small,
        small,
        small,
        pl.BlockSpec(pattern.shape, lambda i: (0, 0)),
        pl.BlockSpec(centers.shape, lambda i: (0, 0)),
        pl.BlockSpec((volumes, size), lambda i: (0, i)),
    ]
    args = [traces, left, right, pattern, centers, observed]
    if not first:
        in_specs += [foot_spec, side_spec]
        args += list(state)
    if final:
        out_specs = [foot_spec]
        out_shape = [jax.ShapeDtypeStruct((comps, flat), bf16)]
        scratch = []
    else:
        out_specs = [foot_spec, side_spec, small]
        out_shape = [
            jax.ShapeDtypeStruct((comps, flat), f32),
            jax.ShapeDtypeStruct((comps, blocks * side_size), f32),
            jax.ShapeDtypeStruct((comps, volumes), f32),
        ]
        scratch = [pltpu.VMEM((comps, volumes), f32), pltpu.VMEM((comps, LANES), f32)]
    return pl.pallas_call(
        functools.partial(sweep_kernel, rows_patch, cols, first, final),
        grid=(blocks,),
        in_specs=in_specs,
        out_specs=out_specs,
        out_shape=out_shape,
        scratch_shapes=scratch,
        compiler_params=pltpu.CompilerParams(vmem_limit_bytes=VMEM_LIMIT),
        name="sweep",
    )(*args)


def from_neighbours(value, axis):
    count = lax.axis_size(axis)
    left = lax.ppermute(value, axis, [(i, i + 1) for i in range(count - 1)])
    right = lax.ppermute(value, axis, [(i + 1, i) for i in range(count - 1)])
    return left, right


def shards(recording, offsets, center_rows, center_cols, decays):
    frames_dev, height, cols = recording.shape
    wide = lax.axis_size("wide")
    narrow = lax.axis_size("narrow")
    rows_patch = height // wide
    ext_width = cols + EDGE
    comps = center_rows.shape[-1]

    head, tail = pack_edges(recording)
    ring = [(i, (i + 1) % narrow) for i in range(narrow)]
    tail = lax.ppermute(tail, "narrow", ring)
    head = lax.ppermute(head, "narrow", [(b, a) for a, b in ring])
    shifts = lax.dynamic_slice_in_dim(offsets, lax.axis_index("wide") * frames_dev, frames_dev, 1)
    core, border = register(shifts, recording, head, tail, wide)
    received = lax.all_to_all(core, "wide", split_axis=0, concat_axis=0, tiled=True)
    border = lax.all_to_all(border, "wide", split_axis=0, concat_axis=0, tiled=True)
    received = received.reshape(wide * frames_dev, rows_patch, cols)

    place = np.arange(GROUP * ext_width)
    row = place // ext_width
    col = place % ext_width - MARGIN
    global_col = lax.axis_index("narrow") * cols + jnp.asarray(col, jnp.int32)
    inside = ((global_col >= 0) & (global_col < cols * narrow)).astype(f32)
    is_left = jnp.asarray(col < MARGIN, f32) * inside
    is_right = jnp.asarray(col >= cols - MARGIN, f32) * inside
    zero = jnp.zeros_like(inside)
    pattern = jnp.stack(
        [jnp.asarray(row, f32), jnp.asarray(col, f32), inside, is_left, is_right, zero, zero, zero]
    )
    centers = jnp.stack([center_rows[0, 0], center_cols[0, 0]], axis=1).astype(f32)
    left, right = from_neighbours(centers, "narrow")
    centers = jnp.concatenate(
        [centers, left, right, jnp.zeros((comps, LANES - 6), f32)], axis=1
    )

    observed, traces = observe(received, border, pattern, centers, frames_dev)
    state = None
    for turn in range(ITERS):
        left, right = from_neighbours(traces, "narrow")
        final = turn == ITERS - 1
        out = sweep(
            traces, left, right, pattern, centers, observed, state, rows_patch, cols, final
        )
        if final:
            footprints = out[0]
        else:
            state, traces = out[:2], out[2]
    previous = jnp.concatenate([jnp.zeros((comps, 1), f32), traces[:, :-1]], axis=1)
    spikes = jnp.maximum(0.0, traces - decays[0, 0][:, None] * previous)
    return (
        footprints.reshape(1, 1, comps, -1),
        traces.reshape(1, 1, comps, VOLUMES),
        spikes.reshape(1, 1, comps, VOLUMES),
    )


def solution(mesh):
    in_specs = (
        P(("parts", "wide"), None, "narrow"),
        P(None, "parts"),
        P(("parts", "wide"), "narrow", None),
        P(("parts", "wide"), "narrow", None),
        P(("parts", "wide"), "narrow", None),
    )
    out_specs = (
        P(("parts", "wide"), "narrow", None, None),
        P(("parts", "wide"), "narrow", None, None),
        P(("parts", "wide"), "narrow", None, None),
    )
    return jax.shard_map(shards, mesh=mesh, in_specs=in_specs, out_specs=out_specs, check_vma=False)
```

```python
import functools

import jax
import jax.numpy as jnp
import numpy as np
from jax import lax
from jax.experimental import pallas as pl
from jax.experimental.pallas import tpu as pltpu
from jax.sharding import PartitionSpec as P

PLANES = 2
VOLUMES = 16
MARGIN = 8
SHIFT_MAX = 4
RADIUS = 12
ITERS = 3
RIDGE = 1.0
EDGE = 2 * MARGIN
LANES = 128
GROUP = 8
STACK = 8
VMEM_LIMIT = 48 * 1024 * 1024

f32 = jnp.float32
bf16 = jnp.bfloat16


def roll_lanes(x, shift):
    shift = shift % x.shape[-1]
    return pltpu.roll(x, shift, 1) if shift else x


def lane_iota(shape):
    return lax.broadcasted_iota(jnp.int32, shape, len(shape) - 1)


def pack_kernel(first_ref, last_ref, head_ref, tail_ref):
    frames, height, _ = first_ref.shape
    lane = lane_iota((height, LANES))
    head = jnp.zeros((height, LANES), f32)
    tail = jnp.zeros((height, LANES), f32)
    for f in range(frames):
        here = (lane >= f * EDGE) & (lane < (f + 1) * EDGE)
        head = jnp.where(here, roll_lanes(first_ref[f].astype(f32), f * EDGE), head)
        tail = jnp.where(here, roll_lanes(last_ref[f].astype(f32), (f + 1) * EDGE), tail)
    head_ref[...] = head.astype(bf16)
    tail_ref[...] = tail.astype(bf16)


def pack_edges(recording):
    frames, height, cols = recording.shape
    out = jax.ShapeDtypeStruct((height, LANES), bf16)
    rows = min(height, 128)
    return pl.pallas_call(
        pack_kernel,
        grid=(height // rows,),
        in_specs=[
            pl.BlockSpec((frames, rows, LANES), lambda i: (0, i, 0)),
            pl.BlockSpec((frames, rows, LANES), lambda i: (0, i, cols // LANES - 1)),
        ],
        out_specs=[pl.BlockSpec((rows, LANES), lambda i: (i, 0))] * 2,
        out_shape=[out, out],
        name="pack_edges",
    )(recording, recording)


def register_kernel(shifts_ref, frame_ref, head_ref, tail_ref, core_ref, border_ref, acc_ref):
    f = pl.program_id(0)
    wide, _, rows_patch, cols = core_ref.shape
    height = wide * rows_patch
    width = cols + LANES
    lane = lane_iota((height, LANES))
    back = lax.rem(LANES - f * EDGE, LANES)
    head = pltpu.roll(head_ref[...].astype(f32), back, 1)
    tail = pltpu.roll(tail_ref[...].astype(f32), lax.rem(back + LANES - EDGE, LANES), 1)
    edge = jnp.where(lane < LANES // 2, head, tail)
    frame = jnp.concatenate([frame_ref[0].astype(f32), edge], axis=1)
    row_move = lax.rem(shifts_ref[0, f] + height, height)
    col_move = lax.rem(shifts_ref[1, f] + width, width)
    frame = pltpu.roll(frame, row_move, 0)
    frame = pltpu.roll(frame, col_move, 1)
    core_ref[...] = frame[:, :cols].astype(bf16).reshape(wide, 1, rows_patch, cols)
    moved = pltpu.roll(frame[:, cols:], lax.rem(f * EDGE + MARGIN, LANES), 1)
    here = (lane >= f * EDGE) & (lane < (f + 1) * EDGE)

    @pl.when(f == 0)
    def _():
        acc_ref[...] = jnp.zeros_like(acc_ref)

    acc_ref[...] = jnp.where(here, moved, acc_ref[...])

    @pl.when(f == pl.num_programs(0) - 1)
    def _():
        border_ref[...] = acc_ref[...].astype(bf16).reshape(border_ref.shape)


def register(shifts, recording, head, tail, wide):
    frames, height, cols = recording.shape
    rows_patch = height // wide
    whole = pl.BlockSpec((height, LANES), lambda f: (0, 0))
    return pl.pallas_call(
        register_kernel,
        grid=(frames,),
        in_specs=[
            pl.BlockSpec(memory_space=pltpu.SMEM),
            pl.BlockSpec((1, height, cols), lambda f: (f, 0, 0)),
            whole,
            whole,
        ],
        out_specs=[
            pl.BlockSpec((wide, 1, rows_patch, cols), lambda f: (0, f, 0, 0)),
            pl.BlockSpec((wide, rows_patch, LANES), lambda f: (0, 0, 0)),
        ],
        out_shape=[
            jax.ShapeDtypeStruct((wide, frames, rows_patch, cols), bf16),
            jax.ShapeDtypeStruct((wide, rows_patch, LANES), bf16),
        ],
        scratch_shapes=[pltpu.VMEM((height, LANES), f32)],
        compiler_params=pltpu.CompilerParams(vmem_limit_bytes=VMEM_LIMIT),
        name="register",
    )(shifts, recording, head, tail)


def bump(position, center):
    return jnp.maximum(0.0, 1.0 - jnp.abs(position - center) * (1.0 / RADIUS))


def lane_pieces(cols):
    return [(j * cols, cols if j < GROUP else LANES) for j in range(GROUP + 1)]


NT = (((1,), (1,)), ((), ()))


def nt_dot(a, b):
    return lax.dot_general(a, b, NT, preferred_element_type=f32)


def observe_kernel(
    mix_ref, recv_ref, border_ref, pattern_ref, centers_ref, obs_ref, traces_ref, proj_ref, energy_ref
):
    volumes, rows, cols = recv_ref.shape
    sources = border_ref.shape[0]
    per_source = volumes // sources
    step = pl.program_id(0) * pl.num_programs(1) + pl.program_id(1)
    last = pl.num_programs(0) * pl.num_programs(1) - 1
    base = (pl.program_id(1) * rows).astype(f32)
    mix = mix_ref[...]

    @pl.when(step == 0)
    def _():
        proj_ref[...] = jnp.zeros_like(proj_ref)
        energy_ref[...] = jnp.zeros_like(energy_ref)

    core = jnp.dot(mix, recv_ref[...].reshape(volumes * rows, cols), preferred_element_type=f32)
    strips = [border_ref[s].astype(f32) for s in range(sources)]
    border = jnp.concatenate(
        [
            roll_lanes(strips[v // per_source], -(v % per_source) * EDGE - MARGIN)
            for v in range(volumes)
        ],
        axis=0,
    ).astype(bf16)
    border = jnp.dot(mix, border, preferred_element_type=f32)
    lane = lane_iota((volumes, LANES))
    center_row = centers_ref[:, 0:1]
    center_col = centers_ref[:, 1:2]
    size = GROUP * (cols + EDGE)
    proj = proj_ref[...]
    energy = energy_ref[...]
    for g in range(rows // GROUP):
        carry = None
        for j, (start, width) in enumerate(lane_pieces(cols)):
            if j < GROUP:
                at = (g * GROUP + j) * volumes
                line = jnp.concatenate(
                    [core[at : at + volumes], border[at : at + volumes]], axis=1
                )
                line = roll_lanes(line, MARGIN + EDGE * j)
                first = line[:, :LANES]
                if carry is not None:
                    first = jnp.where(lane < EDGE * j, carry, first)
                carry = line[:, cols:]
                piece = jnp.concatenate([first, line[:, LANES:cols]], axis=1)
            else:
                piece = carry
            low = piece.astype(bf16)
            obs_ref[:, g * size + start : g * size + start + width] = low
            row = pattern_ref[0:1, start : start + width] + (base + g * GROUP)
            col = pattern_ref[1:2, start : start + width]
            inside = pattern_ref[2:3, start : start + width]
            foot = bump(row, center_row) * (bump(col, center_col) * inside)
            proj = proj + nt_dot(foot.astype(bf16), low)
            square = foot * foot
            for c in range(width // LANES):
                energy = energy + square[:, c * LANES : (c + 1) * LANES]
    proj_ref[...] = proj
    energy_ref[...] = energy

    @pl.when(step == last)
    def _():
        total = jnp.sum(energy, axis=1, keepdims=True) + RIDGE
        traces_ref[...] = jnp.maximum(0.0, proj / total)


def observe(received, border, pattern, centers, frames):
    _, rows_patch, cols = received.shape
    comps = centers.shape[0]
    rows = 16
    blocks = rows_patch // rows
    sources = border.shape[0] // PLANES
    size = GROUP * (cols + EDGE)
    same = np.eye(rows)
    mix = np.einsum("yx,vu->yvux", same, np.eye(VOLUMES) - 1.0 / VOLUMES)
    mix = jnp.asarray(mix.reshape(rows * VOLUMES, VOLUMES * rows), bf16)
    flat = PLANES * rows_patch * (cols + EDGE)
    return pl.pallas_call(
        observe_kernel,
        grid=(PLANES, blocks),
        in_specs=[
            pl.BlockSpec(mix.shape, lambda p, y: (0, 0)),
            pl.BlockSpec((VOLUMES, rows, cols), lambda p, y: (p, y, 0)),
            pl.BlockSpec((sources, rows, LANES), lambda p, y: (p, y, 0)),
            pl.BlockSpec((8, size), lambda p, y: (0, 0)),
            pl.BlockSpec((comps, LANES), lambda p, y: (0, 0)),
        ],
        out_specs=[
            pl.BlockSpec((VOLUMES, rows * (cols + EDGE)), lambda p, y: (0, p * blocks + y)),
            pl.BlockSpec((comps, VOLUMES), lambda p, y: (0, 0)),
        ],
        out_shape=[
            jax.ShapeDtypeStruct((VOLUMES, flat), bf16),
            jax.ShapeDtypeStruct((comps, VOLUMES), f32),
        ],
        scratch_shapes=[pltpu.VMEM((comps, VOLUMES), f32), pltpu.VMEM((comps, LANES), f32)],
        compiler_params=pltpu.CompilerParams(vmem_limit_bytes=VMEM_LIMIT),
        name="observe",
    )(mix, received, border, pattern, centers)


def sweep_kernel(rows_patch, cols, first, final, *refs):
    traces_ref, left_ref, right_ref, pattern_ref, centers_ref, obs_ref = refs[:6]
    refs = refs[6:]
    if not first:
        foot_ref, side_ref = refs[:2]
        refs = refs[2:]
    if final:
        (low_ref,) = refs[:1]
        refs = refs[1:]
    else:
        new_foot_ref, new_side_ref, new_traces_ref = refs[:3]
        refs = refs[3:]
    back_ref, ahead_ref, back_side_ref, ahead_side_ref, scale_ref, side_scale_ref = refs[:6]
    if not final:
        proj_ref, energy_ref = refs[6:]
    size = GROUP * (cols + EDGE)
    side_size = (GROUP + 1) * LANES
    groups = obs_ref.shape[1] // size
    volumes = obs_ref.shape[0]
    comps = traces_ref.shape[0]
    step = pl.program_id(0)

    @pl.when(step == 0)
    def _():
        eye_at = lax.broadcasted_iota(jnp.int32, (volumes, volumes), 0)
        eye_to = lax.broadcasted_iota(jnp.int32, (volumes, volumes), 1)
        eye = (eye_at == eye_to).astype(f32).astype(bf16)

        def spread(value):
            rows, columns = value.shape
            tiled = jnp.concatenate([value] * groups, axis=0)
            tiled = jnp.concatenate([tiled] * groups, axis=1)
            at = lax.broadcasted_iota(jnp.int32, tiled.shape, 0) // rows
            to = lax.broadcasted_iota(jnp.int32, tiled.shape, 1) // columns
            return jnp.where(at == to, tiled, 0.0).astype(bf16)

        for which, ref in enumerate((traces_ref, left_ref, right_ref)):
            full = ref[...]
            low = full.astype(bf16)
            flipped = nt_dot(eye, low)
            ahead = spread(low.astype(f32))
            back = spread(flipped)
            scale = 1.0 / (jnp.sum(full * full, axis=1, keepdims=True) + RIDGE)
            scale = jnp.concatenate([jnp.broadcast_to(scale, (comps, LANES))] * groups, axis=0)
            if which == 0:
                ahead_ref[...] = ahead
                back_ref[...] = back
                scale_ref[...] = scale
            else:
                part = (which - 1) * groups * comps
                ahead_side_ref[part : part + groups * comps, :] = ahead
                back_side_ref[:, part : part + groups * comps] = back
                side_scale_ref[part : part + groups * comps, :] = scale
        if not final:
            proj_ref[...] = jnp.zeros_like(proj_ref)
            energy_ref[...] = jnp.zeros_like(energy_ref)

    back = back_ref[...]
    ahead = ahead_ref[...]
    back_side = back_side_ref[...]
    ahead_side = ahead_side_ref[...]

    def over_lanes(value, width):
        return value if width == LANES else jnp.concatenate([value] * (width // LANES), axis=1)

    def stacked(ref, starts, width):
        return jnp.concatenate([ref[:, s : s + width] for s in starts], axis=0)

    for j, (start, width) in enumerate(lane_pieces(cols)):
        starts = [g * size + start for g in range(groups)]
        side_starts = [g * side_size + j * LANES for g in range(groups)]
        inside = pattern_ref[2:3, start : start + LANES]
        is_left = pattern_ref[3:4, start : start + LANES]
        is_right = pattern_ref[4:5, start : start + LANES]
        obs = stacked(obs_ref, starts, width).astype(f32)
        if first:
            col = pattern_ref[1:2, start : start + width]
            in_all = pattern_ref[2:3, start : start + width]
            col_own = bump(col, centers_ref[:, 1:2]) * in_all
            col = col[:, :LANES]
            col_left = bump(col + cols, centers_ref[:, 3:4]) * is_left
            col_right = bump(col - cols, centers_ref[:, 5:6]) * is_right
            foot, side = [], []
            for g in range(groups):
                base = lax.rem((step * groups + g) * GROUP, rows_patch).astype(f32)
                row = pattern_ref[0:1, start : start + width] + base
                foot.append(bump(row, centers_ref[:, 0:1]) * col_own)
                row = row[:, :LANES]
                side.append(
                    bump(row, centers_ref[:, 2:3]) * col_left
                    + bump(row, centers_ref[:, 4:5]) * col_right
                )
            foot = jnp.concatenate(foot, axis=0)
            side = jnp.concatenate(side, axis=0)
        else:
            foot = stacked(foot_ref, starts, width)
            side = stacked(side_ref, side_starts, LANES)

        def residual(foot_low, side):
            model = jnp.dot(back, foot_low, preferred_element_type=f32)
            sides = jnp.concatenate([side * is_left, side * is_right], axis=0).astype(bf16)
            head = model[:, :LANES] + jnp.dot(back_side, sides, preferred_element_type=f32)
            model = head if width == LANES else jnp.concatenate([head, model[:, LANES:]], axis=1)
            return (obs - model).astype(bf16)

        rest = residual(foot.astype(bf16), side)
        update = jnp.dot(ahead, rest, preferred_element_type=f32) * over_lanes(scale_ref[...], width)
        head = update[:, :LANES] * inside
        update = head if width == LANES else jnp.concatenate([head, update[:, LANES:]], axis=1)
        foot = jnp.maximum(0.0, foot + update)
        foot_low = foot.astype(bf16)
        if final:
            for g, at in enumerate(starts):
                low_ref[:, at : at + width] = foot_low[g * comps : (g + 1) * comps]
            continue
        sides = jnp.dot(ahead_side, rest[:, :LANES], preferred_element_type=f32)
        sides = sides * side_scale_ref[...]
        half = groups * comps
        side = jnp.maximum(0.0, side + is_left * sides[:half] + is_right * sides[half:])
        for g in range(groups):
            part = slice(g * comps, (g + 1) * comps)
            new_foot_ref[:, starts[g] : starts[g] + width] = foot[part]
            new_side_ref[:, side_starts[g] : side_starts[g] + LANES] = side[part]
        proj_ref[...] += nt_dot(foot_low, residual(foot_low, side))
        square = foot * foot
        energy = energy_ref[...]
        for c in range(width // LANES):
            energy = energy + square[:, c * LANES : (c + 1) * LANES]
        energy_ref[...] = energy

    if not final:

        @pl.when(step == pl.num_programs(0) - 1)
        def _():
            energy = jnp.sum(energy_ref[...], axis=1, keepdims=True)
            total = RIDGE
            proj = traces_ref[...] * 0.0
            for g in range(groups):
                part = slice(g * comps, (g + 1) * comps)
                total = total + energy[part]
                proj = proj + proj_ref[part, g * volumes : (g + 1) * volumes]
            new_traces_ref[...] = jnp.maximum(0.0, traces_ref[...] + proj / total)


def sweep(traces, left, right, pattern, centers, observed, state, rows_patch, cols, final):
    comps, volumes = traces.shape
    flat = observed.shape[1]
    groups_all = flat // (GROUP * (cols + EDGE))
    per_block = min(STACK, groups_all)
    blocks = groups_all // per_block
    size = per_block * GROUP * (cols + EDGE)
    side_size = per_block * (GROUP + 1) * LANES
    small = pl.BlockSpec((comps, volumes), lambda i: (0, 0))
    foot_spec = pl.BlockSpec((comps, size), lambda i: (0, i))
    side_spec = pl.BlockSpec((comps, side_size), lambda i: (0, i))
    first = state is None
    in_specs = [
        small,
        small,
        small,
        pl.BlockSpec(pattern.shape, lambda i: (0, 0)),
        pl.BlockSpec(centers.shape, lambda i: (0, 0)),
        pl.BlockSpec((volumes, size), lambda i: (0, i)),
    ]
    args = [traces, left, right, pattern, centers, observed]
    if not first:
        in_specs += [foot_spec, side_spec]
        args += list(state)
    if final:
        out_specs = [foot_spec]
        out_shape = [jax.ShapeDtypeStruct((comps, flat), bf16)]
        scratch = []
    else:
        out_specs = [foot_spec, side_spec, small]
        out_shape = [
            jax.ShapeDtypeStruct((comps, flat), f32),
            jax.ShapeDtypeStruct((comps, blocks * side_size), f32),
            jax.ShapeDtypeStruct((comps, volumes), f32),
        ]
        scratch = [
            pltpu.VMEM((per_block * comps, per_block * volumes), f32),
            pltpu.VMEM((per_block * comps, LANES), f32),
        ]
    tall, flat_tall = per_block * comps, per_block * volumes
    scratch = [
        pltpu.VMEM((flat_tall, tall), bf16),
        pltpu.VMEM((tall, flat_tall), bf16),
        pltpu.VMEM((flat_tall, 2 * tall), bf16),
        pltpu.VMEM((2 * tall, flat_tall), bf16),
        pltpu.VMEM((tall, LANES), f32),
        pltpu.VMEM((2 * tall, LANES), f32),
    ] + scratch
    return pl.pallas_call(
        functools.partial(sweep_kernel, rows_patch, cols, first, final),
        grid=(blocks,),
        in_specs=in_specs,
        out_specs=out_specs,
        out_shape=out_shape,
        scratch_shapes=scratch,
        compiler_params=pltpu.CompilerParams(vmem_limit_bytes=VMEM_LIMIT),
        name="sweep",
    )(*args)


def from_neighbours(value, axis):
    count = lax.axis_size(axis)
    left = lax.ppermute(value, axis, [(i, i + 1) for i in range(count - 1)])
    right = lax.ppermute(value, axis, [(i + 1, i) for i in range(count - 1)])
    return left, right


def shards(recording, offsets, center_rows, center_cols, decays):
    frames_dev, height, cols = recording.shape
    wide = lax.axis_size("wide")
    narrow = lax.axis_size("narrow")
    rows_patch = height // wide
    ext_width = cols + EDGE
    comps = center_rows.shape[-1]

    head, tail = pack_edges(recording)
    ring = [(i, (i + 1) % narrow) for i in range(narrow)]
    tail = lax.ppermute(tail, "narrow", ring)
    head = lax.ppermute(head, "narrow", [(b, a) for a, b in ring])
    shifts = lax.dynamic_slice_in_dim(offsets, lax.axis_index("wide") * frames_dev, frames_dev, 1)
    core, border = register(shifts, recording, head, tail, wide)
    received = lax.all_to_all(core, "wide", split_axis=0, concat_axis=0, tiled=True)
    border = lax.all_to_all(border, "wide", split_axis=0, concat_axis=0, tiled=True)
    received = received.reshape(wide * frames_dev, rows_patch, cols)

    place = np.arange(GROUP * ext_width)
    row = place // ext_width
    col = place % ext_width - MARGIN
    global_col = lax.axis_index("narrow") * cols + jnp.asarray(col, jnp.int32)
    inside = ((global_col >= 0) & (global_col < cols * narrow)).astype(f32)
    is_left = jnp.asarray(col < MARGIN, f32) * inside
    is_right = jnp.asarray(col >= cols - MARGIN, f32) * inside
    zero = jnp.zeros_like(inside)
    pattern = jnp.stack(
        [jnp.asarray(row, f32), jnp.asarray(col, f32), inside, is_left, is_right, zero, zero, zero]
    )
    centers = jnp.stack([center_rows[0, 0], center_cols[0, 0]], axis=1).astype(f32)
    left, right = from_neighbours(centers, "narrow")
    centers = jnp.concatenate(
        [centers, left, right, jnp.zeros((comps, LANES - 6), f32)], axis=1
    )

    observed, traces = observe(received, border, pattern, centers, frames_dev)
    state = None
    for turn in range(ITERS):
        left, right = from_neighbours(traces, "narrow")
        final = turn == ITERS - 1
        out = sweep(
            traces, left, right, pattern, centers, observed, state, rows_patch, cols, final
        )
        if final:
            footprints = out[0]
        else:
            state, traces = out[:2], out[2]
    previous = jnp.concatenate([jnp.zeros((comps, 1), f32), traces[:, :-1]], axis=1)
    spikes = jnp.maximum(0.0, traces - decays[0, 0][:, None] * previous)
    return (
        footprints.reshape(1, 1, comps, -1),
        traces.reshape(1, 1, comps, VOLUMES),
        spikes.reshape(1, 1, comps, VOLUMES),
    )


def solution(mesh):
    in_specs = (
        P(("parts", "wide"), None, "narrow"),
        P(None, "parts"),
        P(("parts", "wide"), "narrow", None),
        P(("parts", "wide"), "narrow", None),
        P(("parts", "wide"), "narrow", None),
    )
    out_specs = (
        P(("parts", "wide"), "narrow", None, None),
        P(("parts", "wide"), "narrow", None, None),
        P(("parts", "wide"), "narrow", None, None),
    )
    return jax.shard_map(shards, mesh=mesh, in_specs=in_specs, out_specs=out_specs, check_vma=False)
```

```python
import functools

import jax
import jax.numpy as jnp
import numpy as np
from jax import lax
from jax.experimental import pallas as pl
from jax.experimental.pallas import tpu as pltpu
from jax.sharding import PartitionSpec as P

PLANES = 2
VOLUMES = 16
MARGIN = 8
SHIFT_MAX = 4
RADIUS = 12
ITERS = 3
RIDGE = 1.0
EDGE = 2 * MARGIN
LANES = 128
GROUP = 8
ROWS = 16
STACK = 8
CHUNKS = 2
VMEM_LIMIT = 48 * 1024 * 1024

f32 = jnp.float32
bf16 = jnp.bfloat16


def roll_lanes(x, shift):
    shift = shift % x.shape[-1]
    return pltpu.roll(x, shift, 1) if shift else x


def lane_iota(shape):
    return lax.broadcasted_iota(jnp.int32, shape, len(shape) - 1)


def pack_kernel(first_ref, last_ref, head_ref, tail_ref):
    frames, height, _ = first_ref.shape
    lane = lane_iota((height, LANES))
    head = jnp.zeros((height, LANES), f32)
    tail = jnp.zeros((height, LANES), f32)
    for f in range(frames):
        here = (lane >= f * EDGE) & (lane < (f + 1) * EDGE)
        head = jnp.where(here, roll_lanes(first_ref[f].astype(f32), f * EDGE), head)
        tail = jnp.where(here, roll_lanes(last_ref[f].astype(f32), (f + 1) * EDGE), tail)
    head_ref[...] = head.astype(bf16)
    tail_ref[...] = tail.astype(bf16)


def pack_edges(recording):
    frames, height, cols = recording.shape
    out = jax.ShapeDtypeStruct((height, LANES), bf16)
    rows = min(height, 128)
    return pl.pallas_call(
        pack_kernel,
        grid=(height // rows,),
        in_specs=[
            pl.BlockSpec((frames, rows, LANES), lambda i: (0, i, 0)),
            pl.BlockSpec((frames, rows, LANES), lambda i: (0, i, cols // LANES - 1)),
        ],
        out_specs=[pl.BlockSpec((rows, LANES), lambda i: (i, 0))] * 2,
        out_shape=[out, out],
        name="pack_edges",
    )(recording, recording)


def extra_rows(rows_chunk, cols):
    return -(-(rows_chunk // ROWS) // (cols // LANES)) * ROWS


def frames_of(ref, rows_chunk, cols):
    return (ref.shape[1] - extra_rows(rows_chunk, cols)) // rows_chunk


def register_kernel(shifts_ref, frame_ref, head_ref, tail_ref, *refs):
    out_refs, acc_ref = refs[:-1], refs[-1]
    f = pl.program_id(0)
    frames = pl.num_programs(0)
    _, height, cols = frame_ref.shape
    wide = out_refs[0].shape[0]
    rows_patch = height // wide
    rows_chunk = rows_patch // len(out_refs)
    across = cols // LANES
    width = cols + LANES
    lane = lane_iota((height, LANES))
    back = lax.rem(LANES - f * EDGE, LANES)
    head = pltpu.roll(head_ref[...].astype(f32), back, 1)
    tail = pltpu.roll(tail_ref[...].astype(f32), lax.rem(back + LANES - EDGE, LANES), 1)
    edge = jnp.where(lane < LANES // 2, head, tail)
    frame = jnp.concatenate([frame_ref[0].astype(f32), edge], axis=1)
    row_move = lax.rem(shifts_ref[0, f] + height, height)
    col_move = lax.rem(shifts_ref[1, f] + width, width)
    frame = pltpu.roll(frame, row_move, 0)
    frame = pltpu.roll(frame, col_move, 1)
    core = frame[:, :cols].astype(bf16).reshape(wide, rows_patch, cols)
    for c, ref in enumerate(out_refs):
        at = pl.ds(pl.multiple_of(f * rows_chunk, ROWS), rows_chunk)
        ref[:, at, :] = core[:, c * rows_chunk : (c + 1) * rows_chunk]
    moved = pltpu.roll(frame[:, cols:], lax.rem(f * EDGE + MARGIN, LANES), 1)
    here = (lane >= f * EDGE) & (lane < (f + 1) * EDGE)

    @pl.when(f == 0)
    def _():
        acc_ref[...] = jnp.zeros_like(acc_ref)

    acc_ref[...] = jnp.where(here, moved, acc_ref[...])

    @pl.when(f == frames - 1)
    def _():
        border = acc_ref[...].astype(bf16).reshape(wide, rows_patch, LANES)
        for c, ref in enumerate(out_refs):
            for k in range(rows_chunk // ROWS):
                at = c * rows_chunk + k * ROWS
                row = frames_of(ref, rows_chunk, cols) * rows_chunk + k // across * ROWS
                lane_at = k % across * LANES
                ref[:, row : row + ROWS, lane_at : lane_at + LANES] = border[:, at : at + ROWS]


def register(shifts, recording, head, tail, wide, chunks):
    frames, height, cols = recording.shape
    rows_chunk = height // wide // chunks
    shape = (wide, frames * rows_chunk + extra_rows(rows_chunk, cols), cols)
    whole = pl.BlockSpec((height, LANES), lambda f: (0, 0))
    return pl.pallas_call(
        register_kernel,
        grid=(frames,),
        in_specs=[
            pl.BlockSpec(memory_space=pltpu.SMEM),
            pl.BlockSpec((1, height, cols), lambda f: (f, 0, 0)),
            whole,
            whole,
        ],
        out_specs=[pl.BlockSpec(shape, lambda f: (0, 0, 0))] * chunks,
        out_shape=[jax.ShapeDtypeStruct(shape, bf16)] * chunks,
        scratch_shapes=[pltpu.VMEM((height, LANES), f32)],
        compiler_params=pltpu.CompilerParams(vmem_limit_bytes=VMEM_LIMIT),
        name="register",
    )(shifts, recording, head, tail)


def bump(position, center):
    return jnp.maximum(0.0, 1.0 - jnp.abs(position - center) * (1.0 / RADIUS))


def lane_pieces(cols):
    return [(j * cols, cols if j < GROUP else LANES) for j in range(GROUP + 1)]


NT = (((1,), (1,)), ((), ()))


def nt_dot(a, b):
    return lax.dot_general(a, b, NT, preferred_element_type=f32)


def observe_kernel(
    chunk, rows_chunk, mix_ref, recv_ref, pattern_ref, centers_ref, proj_in, energy_in, *refs
):
    obs_ref, traces_ref, proj_ref, energy_ref = refs[-4:]
    volumes, rows = VOLUMES, ROWS
    sources, _, cols = recv_ref.shape
    per_source = volumes // sources
    across = cols // LANES
    y = pl.program_id(1)
    step = pl.program_id(0) * pl.num_programs(1) + y
    last = pl.num_programs(0) * pl.num_programs(1) - 1
    base = (chunk * rows_chunk + y * rows).astype(f32)
    mix = mix_ref[...]

    @pl.when(step == 0)
    def _():
        proj_ref[...] = proj_in[...]
        energy_ref[...] = energy_in[...]

    def frame_rows(v):
        row = (v % per_source) * rows_chunk + y * rows
        return recv_ref[v // per_source, pl.ds(pl.multiple_of(row, rows), rows), :]

    border_at = per_source * rows_chunk + y // across * rows
    border_at = pl.ds(pl.multiple_of(border_at, rows), rows)
    lanes_at = pl.ds(pl.multiple_of(lax.rem(y, across) * LANES, LANES), LANES)
    received = jnp.concatenate([frame_rows(v) for v in range(volumes)], axis=0)
    core = jnp.dot(mix, received, preferred_element_type=f32)
    strips = [recv_ref[s, border_at, lanes_at].astype(f32) for s in range(sources)]
    border = jnp.concatenate(
        [
            roll_lanes(strips[v // per_source], -(v % per_source) * EDGE - MARGIN)
            for v in range(volumes)
        ],
        axis=0,
    ).astype(bf16)
    border = jnp.dot(mix, border, preferred_element_type=f32)
    lane = lane_iota((volumes, LANES))
    center_row = centers_ref[:, 0:1]
    center_col = centers_ref[:, 1:2]
    size = GROUP * (cols + EDGE)
    proj = proj_ref[...]
    energy = energy_ref[...]
    for g in range(rows // GROUP):
        carry = None
        for j, (start, width) in enumerate(lane_pieces(cols)):
            if j < GROUP:
                at = (g * GROUP + j) * volumes
                line = jnp.concatenate(
                    [core[at : at + volumes], border[at : at + volumes]], axis=1
                )
                line = roll_lanes(line, MARGIN + EDGE * j)
                first = line[:, :LANES]
                if carry is not None:
                    first = jnp.where(lane < EDGE * j, carry, first)
                carry = line[:, cols:]
                piece = jnp.concatenate([first, line[:, LANES:cols]], axis=1)
            else:
                piece = carry
            low = piece.astype(bf16)
            obs_ref[:, g * size + start : g * size + start + width] = low
            row = pattern_ref[0:1, start : start + width] + (base + g * GROUP)
            col = pattern_ref[1:2, start : start + width]
            inside = pattern_ref[2:3, start : start + width]
            foot = bump(row, center_row) * (bump(col, center_col) * inside)
            proj = proj + nt_dot(foot.astype(bf16), low)
            square = foot * foot
            for c in range(width // LANES):
                energy = energy + square[:, c * LANES : (c + 1) * LANES]
    proj_ref[...] = proj
    energy_ref[...] = energy

    @pl.when(step == last)
    def _():
        total = jnp.sum(energy, axis=1, keepdims=True) + RIDGE
        traces_ref[...] = jnp.maximum(0.0, proj / total)


def observe(received, pattern, centers, earlier, rows_patch, chunk, chunks):
    devices, rows_all, cols = received.shape
    comps = centers.shape[0]
    rows_chunk = rows_patch // chunks
    blocks = rows_chunk // ROWS
    sources = devices // PLANES
    size = GROUP * (cols + EDGE)
    mix = np.einsum("yx,vu->yvux", np.eye(ROWS), np.eye(VOLUMES) - 1.0 / VOLUMES)
    mix = jnp.asarray(mix.reshape(ROWS * VOLUMES, VOLUMES * ROWS), bf16)
    flat = PLANES * rows_patch * (cols + EDGE)
    small = pl.BlockSpec((comps, VOLUMES), lambda p, y: (0, 0))
    wide_small = pl.BlockSpec((comps, LANES), lambda p, y: (0, 0))
    if earlier is None:
        rest = [jnp.zeros((comps, VOLUMES), f32), jnp.zeros((comps, LANES), f32)]
        aliases = {}
    else:
        rest = [earlier[2], earlier[3], earlier[0]]
        aliases = {6: 0}
    return pl.pallas_call(
        functools.partial(observe_kernel, chunk, rows_chunk),
        grid=(PLANES, blocks),
        in_specs=[
            pl.BlockSpec(mix.shape, lambda p, y: (0, 0)),
            pl.BlockSpec((sources, rows_all, cols), lambda p, y: (p, 0, 0)),
            pl.BlockSpec((8, size), lambda p, y: (0, 0)),
            wide_small,
            small,
            wide_small,
        ]
        + [pl.BlockSpec(memory_space=pl.ANY)] * len(aliases),
        out_specs=[
            pl.BlockSpec(
                (VOLUMES, ROWS * (cols + EDGE)),
                lambda p, y: (0, (p * chunks + chunk) * blocks + y),
            ),
            small,
            small,
            wide_small,
        ],
        out_shape=[
            jax.ShapeDtypeStruct((VOLUMES, flat), bf16),
            jax.ShapeDtypeStruct((comps, VOLUMES), f32),
            jax.ShapeDtypeStruct((comps, VOLUMES), f32),
            jax.ShapeDtypeStruct((comps, LANES), f32),
        ],
        input_output_aliases=aliases,
        compiler_params=pltpu.CompilerParams(vmem_limit_bytes=VMEM_LIMIT),
        name="observe",
    )(mix, received, pattern, centers, *rest)


def sweep_kernel(rows_patch, cols, first, final, *refs):
    traces_ref, left_ref, right_ref, pattern_ref, centers_ref, obs_ref = refs[:6]
    refs = refs[6:]
    if not first:
        foot_ref, side_ref = refs[:2]
        refs = refs[2:]
    if final:
        (low_ref,) = refs[:1]
        refs = refs[1:]
    else:
        new_foot_ref, new_side_ref, new_traces_ref = refs[:3]
        refs = refs[3:]
    back_ref, ahead_ref, back_side_ref, ahead_side_ref, scale_ref, side_scale_ref = refs[:6]
    if not final:
        proj_ref, energy_ref = refs[6:]
    size = GROUP * (cols + EDGE)
    side_size = (GROUP + 1) * LANES
    groups = obs_ref.shape[1] // size
    volumes = obs_ref.shape[0]
    comps = traces_ref.shape[0]
    step = pl.program_id(0)

    @pl.when(step == 0)
    def _():
        eye_at = lax.broadcasted_iota(jnp.int32, (volumes, volumes), 0)
        eye_to = lax.broadcasted_iota(jnp.int32, (volumes, volumes), 1)
        eye = (eye_at == eye_to).astype(f32).astype(bf16)

        def spread(value):
            rows, columns = value.shape
            tiled = jnp.concatenate([value] * groups, axis=0)
            tiled = jnp.concatenate([tiled] * groups, axis=1)
            at = lax.broadcasted_iota(jnp.int32, tiled.shape, 0) // rows
            to = lax.broadcasted_iota(jnp.int32, tiled.shape, 1) // columns
            return jnp.where(at == to, tiled, 0.0).astype(bf16)

        for which, ref in enumerate((traces_ref, left_ref, right_ref)):
            full = ref[...]
            low = full.astype(bf16)
            flipped = nt_dot(eye, low)
            ahead = spread(low.astype(f32))
            back = spread(flipped)
            scale = 1.0 / (jnp.sum(full * full, axis=1, keepdims=True) + RIDGE)
            scale = jnp.concatenate([jnp.broadcast_to(scale, (comps, LANES))] * groups, axis=0)
            if which == 0:
                ahead_ref[...] = ahead
                back_ref[...] = back
                scale_ref[...] = scale
            else:
                part = (which - 1) * groups * comps
                ahead_side_ref[part : part + groups * comps, :] = ahead
                back_side_ref[:, part : part + groups * comps] = back
                side_scale_ref[part : part + groups * comps, :] = scale
        if not final:
            proj_ref[...] = jnp.zeros_like(proj_ref)
            energy_ref[...] = jnp.zeros_like(energy_ref)

    back = back_ref[...]
    ahead = ahead_ref[...]
    back_side = back_side_ref[...]
    ahead_side = ahead_side_ref[...]

    def over_lanes(value, width):
        return value if width == LANES else jnp.concatenate([value] * (width // LANES), axis=1)

    def stacked(ref, starts, width):
        return jnp.concatenate([ref[:, s : s + width] for s in starts], axis=0)

    for j, (start, width) in enumerate(lane_pieces(cols)):
        starts = [g * size + start for g in range(groups)]
        side_starts = [g * side_size + j * LANES for g in range(groups)]
        inside = pattern_ref[2:3, start : start + LANES]
        is_left = pattern_ref[3:4, start : start + LANES]
        is_right = pattern_ref[4:5, start : start + LANES]
        obs = stacked(obs_ref, starts, width).astype(f32)
        if first:
            col = pattern_ref[1:2, start : start + width]
            in_all = pattern_ref[2:3, start : start + width]
            col_own = bump(col, centers_ref[:, 1:2]) * in_all
            col = col[:, :LANES]
            col_left = bump(col + cols, centers_ref[:, 3:4]) * is_left
            col_right = bump(col - cols, centers_ref[:, 5:6]) * is_right
            foot, side = [], []
            for g in range(groups):
                base = lax.rem((step * groups + g) * GROUP, rows_patch).astype(f32)
                row = pattern_ref[0:1, start : start + width] + base
                foot.append(bump(row, centers_ref[:, 0:1]) * col_own)
                row = row[:, :LANES]
                side.append(
                    bump(row, centers_ref[:, 2:3]) * col_left
                    + bump(row, centers_ref[:, 4:5]) * col_right
                )
            foot = jnp.concatenate(foot, axis=0)
            side = jnp.concatenate(side, axis=0)
        else:
            foot = stacked(foot_ref, starts, width)
            side = stacked(side_ref, side_starts, LANES)

        def residual(foot_low, side):
            model = jnp.dot(back, foot_low, preferred_element_type=f32)
            sides = jnp.concatenate([side * is_left, side * is_right], axis=0).astype(bf16)
            head = model[:, :LANES] + jnp.dot(back_side, sides, preferred_element_type=f32)
            model = head if width == LANES else jnp.concatenate([head, model[:, LANES:]], axis=1)
            return (obs - model).astype(bf16)

        rest = residual(foot.astype(bf16), side)
        update = jnp.dot(ahead, rest, preferred_element_type=f32) * over_lanes(scale_ref[...], width)
        head = update[:, :LANES] * inside
        update = head if width == LANES else jnp.concatenate([head, update[:, LANES:]], axis=1)
        foot = jnp.maximum(0.0, foot + update)
        foot_low = foot.astype(bf16)
        if final:
            for g, at in enumerate(starts):
                low_ref[:, at : at + width] = foot_low[g * comps : (g + 1) * comps]
            continue
        sides = jnp.dot(ahead_side, rest[:, :LANES], preferred_element_type=f32)
        sides = sides * side_scale_ref[...]
        half = groups * comps
        side = jnp.maximum(0.0, side + is_left * sides[:half] + is_right * sides[half:])
        for g in range(groups):
            part = slice(g * comps, (g + 1) * comps)
            new_foot_ref[:, starts[g] : starts[g] + width] = foot[part]
            new_side_ref[:, side_starts[g] : side_starts[g] + LANES] = side[part]
        proj_ref[...] += nt_dot(foot_low, residual(foot_low, side))
        square = foot * foot
        energy = energy_ref[...]
        for c in range(width // LANES):
            energy = energy + square[:, c * LANES : (c + 1) * LANES]
        energy_ref[...] = energy

    if not final:

        @pl.when(step == pl.num_programs(0) - 1)
        def _():
            energy = jnp.sum(energy_ref[...], axis=1, keepdims=True)
            total = RIDGE
            proj = traces_ref[...] * 0.0
            for g in range(groups):
                part = slice(g * comps, (g + 1) * comps)
                total = total + energy[part]
                proj = proj + proj_ref[part, g * volumes : (g + 1) * volumes]
            new_traces_ref[...] = jnp.maximum(0.0, traces_ref[...] + proj / total)


def sweep(traces, left, right, pattern, centers, observed, state, rows_patch, cols, final):
    comps, volumes = traces.shape
    flat = observed.shape[1]
    groups_all = flat // (GROUP * (cols + EDGE))
    per_block = min(STACK, groups_all)
    blocks = groups_all // per_block
    size = per_block * GROUP * (cols + EDGE)
    side_size = per_block * (GROUP + 1) * LANES
    small = pl.BlockSpec((comps, volumes), lambda i: (0, 0))
    foot_spec = pl.BlockSpec((comps, size), lambda i: (0, i))
    side_spec = pl.BlockSpec((comps, side_size), lambda i: (0, i))
    first = state is None
    in_specs = [
        small,
        small,
        small,
        pl.BlockSpec(pattern.shape, lambda i: (0, 0)),
        pl.BlockSpec(centers.shape, lambda i: (0, 0)),
        pl.BlockSpec((volumes, size), lambda i: (0, i)),
    ]
    args = [traces, left, right, pattern, centers, observed]
    if not first:
        in_specs += [foot_spec, side_spec]
        args += list(state)
    if final:
        out_specs = [foot_spec]
        out_shape = [jax.ShapeDtypeStruct((comps, flat), bf16)]
        scratch = []
    else:
        out_specs = [foot_spec, side_spec, small]
        out_shape = [
            jax.ShapeDtypeStruct((comps, flat), f32),
            jax.ShapeDtypeStruct((comps, blocks * side_size), f32),
            jax.ShapeDtypeStruct((comps, volumes), f32),
        ]
        scratch = [
            pltpu.VMEM((per_block * comps, per_block * volumes), f32),
            pltpu.VMEM((per_block * comps, LANES), f32),
        ]
    tall, flat_tall = per_block * comps, per_block * volumes
    scratch = [
        pltpu.VMEM((flat_tall, tall), bf16),
        pltpu.VMEM((tall, flat_tall), bf16),
        pltpu.VMEM((flat_tall, 2 * tall), bf16),
        pltpu.VMEM((2 * tall, flat_tall), bf16),
        pltpu.VMEM((tall, LANES), f32),
        pltpu.VMEM((2 * tall, LANES), f32),
    ] + scratch
    return pl.pallas_call(
        functools.partial(sweep_kernel, rows_patch, cols, first, final),
        grid=(blocks,),
        in_specs=in_specs,
        out_specs=out_specs,
        out_shape=out_shape,
        scratch_shapes=scratch,
        compiler_params=pltpu.CompilerParams(vmem_limit_bytes=VMEM_LIMIT),
        name="sweep",
    )(*args)


def from_neighbours(value, axis):
    count = lax.axis_size(axis)
    left = lax.ppermute(value, axis, [(i, i + 1) for i in range(count - 1)])
    right = lax.ppermute(value, axis, [(i + 1, i) for i in range(count - 1)])
    return left, right


def shards(recording, offsets, center_rows, center_cols, decays):
    frames_dev, height, cols = recording.shape
    wide = lax.axis_size("wide")
    narrow = lax.axis_size("narrow")
    rows_patch = height // wide
    ext_width = cols + EDGE
    comps = center_rows.shape[-1]

    head, tail = pack_edges(recording)
    ring = [(i, (i + 1) % narrow) for i in range(narrow)]
    tail = lax.ppermute(tail, "narrow", ring)
    head = lax.ppermute(head, "narrow", [(b, a) for a, b in ring])
    shifts = lax.dynamic_slice_in_dim(offsets, lax.axis_index("wide") * frames_dev, frames_dev, 1)
    chunks = CHUNKS if rows_patch % (CHUNKS * ROWS) == 0 else 1
    received = [
        lax.all_to_all(part, "wide", split_axis=0, concat_axis=0, tiled=True)
        for part in register(shifts, recording, head, tail, wide, chunks)
    ]

    place = np.arange(GROUP * ext_width)
    row = place // ext_width
    col = place % ext_width - MARGIN
    global_col = lax.axis_index("narrow") * cols + jnp.asarray(col, jnp.int32)
    inside = ((global_col >= 0) & (global_col < cols * narrow)).astype(f32)
    is_left = jnp.asarray(col < MARGIN, f32) * inside
    is_right = jnp.asarray(col >= cols - MARGIN, f32) * inside
    zero = jnp.zeros_like(inside)
    pattern = jnp.stack(
        [jnp.asarray(row, f32), jnp.asarray(col, f32), inside, is_left, is_right, zero, zero, zero]
    )
    centers = jnp.stack([center_rows[0, 0], center_cols[0, 0]], axis=1).astype(f32)
    left, right = from_neighbours(centers, "narrow")
    centers = jnp.concatenate(
        [centers, left, right, jnp.zeros((comps, LANES - 6), f32)], axis=1
    )

    earlier = None
    for chunk in range(chunks):
        earlier = observe(received[chunk], pattern, centers, earlier, rows_patch, chunk, chunks)
    observed, traces = earlier[:2]
    state = None
    for turn in range(ITERS):
        left, right = from_neighbours(traces, "narrow")
        final = turn == ITERS - 1
        out = sweep(
            traces, left, right, pattern, centers, observed, state, rows_patch, cols, final
        )
        if final:
            footprints = out[0]
        else:
            state, traces = out[:2], out[2]
    previous = jnp.concatenate([jnp.zeros((comps, 1), f32), traces[:, :-1]], axis=1)
    spikes = jnp.maximum(0.0, traces - decays[0, 0][:, None] * previous)
    return (
        footprints.reshape(1, 1, comps, -1),
        traces.reshape(1, 1, comps, VOLUMES),
        spikes.reshape(1, 1, comps, VOLUMES),
    )


def solution(mesh):
    in_specs = (
        P(("parts", "wide"), None, "narrow"),
        P(None, "parts"),
        P(("parts", "wide"), "narrow", None),
        P(("parts", "wide"), "narrow", None),
        P(("parts", "wide"), "narrow", None),
    )
    out_specs = (
        P(("parts", "wide"), "narrow", None, None),
        P(("parts", "wide"), "narrow", None, None),
        P(("parts", "wide"), "narrow", None, None),
    )
    return jax.shard_map(shards, mesh=mesh, in_specs=in_specs, out_specs=out_specs, check_vma=False)
```

```python
import functools

import jax
import jax.numpy as jnp
import numpy as np
from jax import lax
from jax.experimental import pallas as pl
from jax.experimental.pallas import tpu as pltpu
from jax.sharding import PartitionSpec as P

PLANES = 2
VOLUMES = 16
MARGIN = 8
SHIFT_MAX = 4
RADIUS = 12
ITERS = 3
RIDGE = 1.0
EDGE = 2 * MARGIN
LANES = 128
GROUP = 8
ROWS = 16
STACK = 8
CHUNKS = 2
VMEM_LIMIT = 48 * 1024 * 1024

f32 = jnp.float32
bf16 = jnp.bfloat16


def roll_lanes(x, shift):
    shift = shift % x.shape[-1]
    return pltpu.roll(x, shift, 1) if shift else x


def lane_iota(shape):
    return lax.broadcasted_iota(jnp.int32, shape, len(shape) - 1)


def pack_kernel(first_ref, last_ref, head_ref, tail_ref):
    frames, height, _ = first_ref.shape
    lane = lane_iota((height, LANES))
    head = jnp.zeros((height, LANES), f32)
    tail = jnp.zeros((height, LANES), f32)
    for f in range(frames):
        here = (lane >= f * EDGE) & (lane < (f + 1) * EDGE)
        head = jnp.where(here, roll_lanes(first_ref[f].astype(f32), f * EDGE), head)
        tail = jnp.where(here, roll_lanes(last_ref[f].astype(f32), (f + 1) * EDGE), tail)
    head_ref[...] = head.astype(bf16)
    tail_ref[...] = tail.astype(bf16)


def pack_edges(recording):
    frames, height, cols = recording.shape
    out = jax.ShapeDtypeStruct((height, LANES), bf16)
    rows = min(height, 128)
    return pl.pallas_call(
        pack_kernel,
        grid=(height // rows,),
        in_specs=[
            pl.BlockSpec((frames, rows, LANES), lambda i: (0, i, 0)),
            pl.BlockSpec((frames, rows, LANES), lambda i: (0, i, cols // LANES - 1)),
        ],
        out_specs=[pl.BlockSpec((rows, LANES), lambda i: (i, 0))] * 2,
        out_shape=[out, out],
        name="pack_edges",
    )(recording, recording)


def extra_rows(rows_chunk, cols):
    return -(-(rows_chunk // ROWS) // (cols // LANES)) * ROWS


def frames_of(ref, rows_chunk, cols):
    return (ref.shape[1] - extra_rows(rows_chunk, cols)) // rows_chunk


def register_kernel(shifts_ref, frame_ref, head_ref, tail_ref, *refs):
    out_refs, acc_ref = refs[:-1], refs[-1]
    f = pl.program_id(0)
    frames = pl.num_programs(0)
    _, height, cols = frame_ref.shape
    wide = out_refs[0].shape[0]
    rows_patch = height // wide
    rows_chunk = rows_patch // len(out_refs)
    across = cols // LANES
    width = cols + LANES
    lane = lane_iota((height, LANES))
    back = lax.rem(LANES - f * EDGE, LANES)
    head = pltpu.roll(head_ref[...].astype(f32), back, 1)
    tail = pltpu.roll(tail_ref[...].astype(f32), lax.rem(back + LANES - EDGE, LANES), 1)
    edge = jnp.where(lane < LANES // 2, head, tail)
    frame = jnp.concatenate([frame_ref[0].astype(f32), edge], axis=1)
    row_move = lax.rem(shifts_ref[0, f] + height, height)
    col_move = lax.rem(shifts_ref[1, f] + width, width)
    frame = pltpu.roll(frame, row_move, 0)
    frame = pltpu.roll(frame, col_move, 1)
    core = frame[:, :cols].astype(bf16).reshape(wide, rows_patch, cols)
    for c, ref in enumerate(out_refs):
        at = pl.ds(pl.multiple_of(f * rows_chunk, ROWS), rows_chunk)
        ref[:, at, :] = core[:, c * rows_chunk : (c + 1) * rows_chunk]
    moved = pltpu.roll(frame[:, cols:], lax.rem(f * EDGE + MARGIN, LANES), 1)
    here = (lane >= f * EDGE) & (lane < (f + 1) * EDGE)

    @pl.when(f == 0)
    def _():
        acc_ref[...] = jnp.zeros_like(acc_ref)

    acc_ref[...] = jnp.where(here, moved, acc_ref[...])

    @pl.when(f == frames - 1)
    def _():
        border = acc_ref[...].astype(bf16).reshape(wide, rows_patch, LANES)
        for c, ref in enumerate(out_refs):
            for k in range(rows_chunk // ROWS):
                at = c * rows_chunk + k * ROWS
                row = frames_of(ref, rows_chunk, cols) * rows_chunk + k // across * ROWS
                lane_at = k % across * LANES
                ref[:, row : row + ROWS, lane_at : lane_at + LANES] = border[:, at : at + ROWS]


def register(shifts, recording, head, tail, wide, chunks):
    frames, height, cols = recording.shape
    rows_chunk = height // wide // chunks
    shape = (wide, frames * rows_chunk + extra_rows(rows_chunk, cols), cols)
    whole = pl.BlockSpec((height, LANES), lambda f: (0, 0))
    return pl.pallas_call(
        register_kernel,
        grid=(frames,),
        in_specs=[
            pl.BlockSpec(memory_space=pltpu.SMEM),
            pl.BlockSpec((1, height, cols), lambda f: (f, 0, 0)),
            whole,
            whole,
        ],
        out_specs=[pl.BlockSpec(shape, lambda f: (0, 0, 0))] * chunks,
        out_shape=[jax.ShapeDtypeStruct(shape, bf16)] * chunks,
        scratch_shapes=[pltpu.VMEM((height, LANES), f32)],
        compiler_params=pltpu.CompilerParams(vmem_limit_bytes=VMEM_LIMIT),
        name="register",
    )(shifts, recording, head, tail)


def bump(position, center):
    return jnp.maximum(0.0, 1.0 - jnp.abs(position - center) * (1.0 / RADIUS))


def lane_pieces(cols):
    return [(j * cols, cols if j < GROUP else LANES) for j in range(GROUP + 1)]


NT = (((1,), (1,)), ((), ()))


def nt_dot(a, b):
    return lax.dot_general(a, b, NT, preferred_element_type=f32)


def observe_kernel(
    chunk, rows_chunk, mix_ref, recv_ref, pattern_ref, centers_ref, proj_in, energy_in, *refs
):
    obs_ref, traces_ref, proj_ref, energy_ref = refs[-4:]
    volumes, rows = VOLUMES, ROWS
    sources, _, cols = recv_ref.shape
    per_source = volumes // sources
    across = cols // LANES
    y = pl.program_id(1)
    step = pl.program_id(0) * pl.num_programs(1) + y
    last = pl.num_programs(0) * pl.num_programs(1) - 1
    base = (chunk * rows_chunk + y * rows).astype(f32)
    mix = mix_ref[...]

    @pl.when(step == 0)
    def _():
        proj_ref[...] = proj_in[...]
        energy_ref[...] = energy_in[...]

    def frame_rows(v):
        row = (v % per_source) * rows_chunk + y * rows
        return recv_ref[v // per_source, pl.ds(pl.multiple_of(row, rows), rows), :]

    border_at = per_source * rows_chunk + y // across * rows
    border_at = pl.ds(pl.multiple_of(border_at, rows), rows)
    lanes_at = pl.ds(pl.multiple_of(lax.rem(y, across) * LANES, LANES), LANES)
    received = jnp.concatenate([frame_rows(v) for v in range(volumes)], axis=0)
    core = jnp.dot(mix, received, preferred_element_type=f32)
    strips = [recv_ref[s, border_at, lanes_at].astype(f32) for s in range(sources)]
    border = jnp.concatenate(
        [
            roll_lanes(strips[v // per_source], -(v % per_source) * EDGE - MARGIN)
            for v in range(volumes)
        ],
        axis=0,
    ).astype(bf16)
    border = jnp.dot(mix, border, preferred_element_type=f32)
    lane = lane_iota((volumes, LANES))
    center_row = centers_ref[:, 0:1]
    center_col = centers_ref[:, 1:2]
    size = GROUP * (cols + EDGE)
    proj = proj_ref[...]
    energy = energy_ref[...]
    for g in range(rows // GROUP):
        carry = None
        for j, (start, width) in enumerate(lane_pieces(cols)):
            if j < GROUP:
                at = (g * GROUP + j) * volumes
                line = jnp.concatenate(
                    [core[at : at + volumes], border[at : at + volumes]], axis=1
                )
                line = roll_lanes(line, MARGIN + EDGE * j)
                first = line[:, :LANES]
                if carry is not None:
                    first = jnp.where(lane < EDGE * j, carry, first)
                carry = line[:, cols:]
                piece = jnp.concatenate([first, line[:, LANES:cols]], axis=1)
            else:
                piece = carry
            low = piece.astype(bf16)
            obs_ref[:, g * size + start : g * size + start + width] = low
            row = pattern_ref[0:1, start : start + width] + (base + g * GROUP)
            col = pattern_ref[1:2, start : start + width]
            inside = pattern_ref[2:3, start : start + width]
            foot = bump(row, center_row) * (bump(col, center_col) * inside)
            proj = proj + nt_dot(foot.astype(bf16), low)
            square = foot * foot
            for c in range(width // LANES):
                energy = energy + square[:, c * LANES : (c + 1) * LANES]
    proj_ref[...] = proj
    energy_ref[...] = energy

    @pl.when(step == last)
    def _():
        total = jnp.sum(energy, axis=1, keepdims=True) + RIDGE
        traces_ref[...] = jnp.maximum(0.0, proj / total)


def observe(received, pattern, centers, earlier, rows_patch, chunk, chunks):
    devices, rows_all, cols = received.shape
    comps = centers.shape[0]
    rows_chunk = rows_patch // chunks
    blocks = rows_chunk // ROWS
    sources = devices // PLANES
    size = GROUP * (cols + EDGE)
    mix = np.einsum("yx,vu->yvux", np.eye(ROWS), np.eye(VOLUMES) - 1.0 / VOLUMES)
    mix = jnp.asarray(mix.reshape(ROWS * VOLUMES, VOLUMES * ROWS), bf16)
    flat = PLANES * rows_patch * (cols + EDGE)
    small = pl.BlockSpec((comps, VOLUMES), lambda p, y: (0, 0))
    wide_small = pl.BlockSpec((comps, LANES), lambda p, y: (0, 0))
    if earlier is None:
        rest = [jnp.zeros((comps, VOLUMES), f32), jnp.zeros((comps, LANES), f32)]
        aliases = {}
    else:
        rest = [earlier[2], earlier[3], earlier[0]]
        aliases = {6: 0}
    return pl.pallas_call(
        functools.partial(observe_kernel, chunk, rows_chunk),
        grid=(PLANES, blocks),
        in_specs=[
            pl.BlockSpec(mix.shape, lambda p, y: (0, 0)),
            pl.BlockSpec((sources, rows_all, cols), lambda p, y: (p, 0, 0)),
            pl.BlockSpec((8, size), lambda p, y: (0, 0)),
            wide_small,
            small,
            wide_small,
        ]
        + [pl.BlockSpec(memory_space=pl.ANY)] * len(aliases),
        out_specs=[
            pl.BlockSpec(
                (VOLUMES, ROWS * (cols + EDGE)),
                lambda p, y: (0, (p * chunks + chunk) * blocks + y),
            ),
            small,
            small,
            wide_small,
        ],
        out_shape=[
            jax.ShapeDtypeStruct((VOLUMES, flat), bf16),
            jax.ShapeDtypeStruct((comps, VOLUMES), f32),
            jax.ShapeDtypeStruct((comps, VOLUMES), f32),
            jax.ShapeDtypeStruct((comps, LANES), f32),
        ],
        input_output_aliases=aliases,
        compiler_params=pltpu.CompilerParams(vmem_limit_bytes=VMEM_LIMIT),
        name="observe",
    )(mix, received, pattern, centers, *rest)


def sweep_kernel(rows_patch, cols, first, final, *refs):
    traces_ref, left_ref, right_ref, pattern_ref, centers_ref, obs_ref = refs[:6]
    refs = refs[6:]
    if not first:
        foot_ref, side_ref = refs[:2]
        refs = refs[2:]
    if final:
        (low_ref,) = refs[:1]
        refs = refs[1:]
    else:
        new_foot_ref, new_side_ref, new_traces_ref = refs[:3]
        refs = refs[3:]
    back_ref, ahead_ref, back_side_ref, ahead_side_ref, scale_ref, side_scale_ref = refs[:6]
    if not final:
        proj_ref, energy_ref = refs[6:]
    size = GROUP * (cols + EDGE)
    side_size = (GROUP + 1) * LANES
    groups = obs_ref.shape[1] // size
    volumes = obs_ref.shape[0]
    comps = traces_ref.shape[0]
    step = pl.program_id(0)

    @pl.when(step == 0)
    def _():
        eye_at = lax.broadcasted_iota(jnp.int32, (volumes, volumes), 0)
        eye_to = lax.broadcasted_iota(jnp.int32, (volumes, volumes), 1)
        eye = (eye_at == eye_to).astype(f32).astype(bf16)

        def spread(value):
            rows, columns = value.shape
            tiled = jnp.concatenate([value] * groups, axis=0)
            tiled = jnp.concatenate([tiled] * groups, axis=1)
            at = lax.broadcasted_iota(jnp.int32, tiled.shape, 0) // rows
            to = lax.broadcasted_iota(jnp.int32, tiled.shape, 1) // columns
            return jnp.where(at == to, tiled, 0.0).astype(bf16)

        for which, ref in enumerate((traces_ref, left_ref, right_ref)):
            full = ref[...]
            low = full.astype(bf16)
            flipped = nt_dot(eye, low)
            ahead = spread(low.astype(f32))
            back = spread(flipped)
            scale = 1.0 / (jnp.sum(full * full, axis=1, keepdims=True) + RIDGE)
            scale = jnp.concatenate([jnp.broadcast_to(scale, (comps, LANES))] * groups, axis=0)
            if which == 0:
                ahead_ref[...] = ahead
                back_ref[...] = back
                scale_ref[...] = scale
            else:
                part = (which - 1) * groups * comps
                ahead_side_ref[part : part + groups * comps, :] = ahead
                back_side_ref[:, part : part + groups * comps] = back
                side_scale_ref[part : part + groups * comps, :] = scale
        if not final:
            proj_ref[...] = jnp.zeros_like(proj_ref)
            energy_ref[...] = jnp.zeros_like(energy_ref)

    back = back_ref[...]
    ahead = ahead_ref[...]
    back_side = back_side_ref[...]
    ahead_side = ahead_side_ref[...]

    def over_lanes(value, width):
        return value if width == LANES else jnp.concatenate([value] * (width // LANES), axis=1)

    def stacked(ref, starts, width):
        return jnp.concatenate([ref[:, s : s + width] for s in starts], axis=0)

    for j, (start, width) in enumerate(lane_pieces(cols)):
        starts = [g * size + start for g in range(groups)]
        side_starts = [g * side_size + j * LANES for g in range(groups)]
        inside = pattern_ref[2:3, start : start + LANES]
        is_left = pattern_ref[3:4, start : start + LANES]
        is_right = pattern_ref[4:5, start : start + LANES]
        obs = stacked(obs_ref, starts, width).astype(f32)
        if first:
            col = pattern_ref[1:2, start : start + width]
            in_all = pattern_ref[2:3, start : start + width]
            col_own = bump(col, centers_ref[:, 1:2]) * in_all
            col = col[:, :LANES]
            col_left = bump(col + cols, centers_ref[:, 3:4]) * is_left
            col_right = bump(col - cols, centers_ref[:, 5:6]) * is_right
            foot, side = [], []
            for g in range(groups):
                base = lax.rem((step * groups + g) * GROUP, rows_patch).astype(f32)
                row = pattern_ref[0:1, start : start + width] + base
                foot.append(bump(row, centers_ref[:, 0:1]) * col_own)
                row = row[:, :LANES]
                side.append(
                    bump(row, centers_ref[:, 2:3]) * col_left
                    + bump(row, centers_ref[:, 4:5]) * col_right
                )
            foot = jnp.concatenate(foot, axis=0)
            side = jnp.concatenate(side, axis=0)
        else:
            foot = stacked(foot_ref, starts, width)
            side = stacked(side_ref, side_starts, LANES)

        def residual(foot_low, side):
            model = jnp.dot(back, foot_low, preferred_element_type=f32)
            sides = jnp.concatenate([side * is_left, side * is_right], axis=0).astype(bf16)
            head = model[:, :LANES] + jnp.dot(back_side, sides, preferred_element_type=f32)
            model = head if width == LANES else jnp.concatenate([head, model[:, LANES:]], axis=1)
            return (obs - model).astype(bf16)

        rest = residual(foot.astype(bf16), side)
        update = jnp.dot(ahead, rest, preferred_element_type=f32) * over_lanes(scale_ref[...], width)
        head = update[:, :LANES] * inside
        update = head if width == LANES else jnp.concatenate([head, update[:, LANES:]], axis=1)
        foot = jnp.maximum(0.0, foot + update)
        foot_low = foot.astype(bf16)
        if final:
            for g, at in enumerate(starts):
                low_ref[:, at : at + width] = foot_low[g * comps : (g + 1) * comps]
            continue
        sides = jnp.dot(ahead_side, rest[:, :LANES], preferred_element_type=f32)
        sides = sides * side_scale_ref[...]
        half = groups * comps
        side = jnp.maximum(0.0, side + is_left * sides[:half] + is_right * sides[half:])
        for g in range(groups):
            part = slice(g * comps, (g + 1) * comps)
            new_foot_ref[:, starts[g] : starts[g] + width] = foot[part]
            new_side_ref[:, side_starts[g] : side_starts[g] + LANES] = side[part]
        proj_ref[...] += nt_dot(foot_low, residual(foot_low, side))
        square = foot * foot
        energy = energy_ref[...]
        for c in range(width // LANES):
            energy = energy + square[:, c * LANES : (c + 1) * LANES]
        energy_ref[...] = energy

    if not final:

        @pl.when(step == pl.num_programs(0) - 1)
        def _():
            energy = jnp.sum(energy_ref[...], axis=1, keepdims=True)
            total = RIDGE
            proj = traces_ref[...] * 0.0
            for g in range(groups):
                part = slice(g * comps, (g + 1) * comps)
                total = total + energy[part]
                proj = proj + proj_ref[part, g * volumes : (g + 1) * volumes]
            new_traces_ref[...] = jnp.maximum(0.0, traces_ref[...] + proj / total)


def sweep(traces, left, right, pattern, centers, observed, state, rows_patch, cols, final):
    comps, volumes = traces.shape
    flat = observed.shape[1]
    groups_all = flat // (GROUP * (cols + EDGE))
    per_block = min(STACK, groups_all)
    blocks = groups_all // per_block
    size = per_block * GROUP * (cols + EDGE)
    side_size = per_block * (GROUP + 1) * LANES
    small = pl.BlockSpec((comps, volumes), lambda i: (0, 0))
    foot_spec = pl.BlockSpec((comps, size), lambda i: (0, i))
    side_spec = pl.BlockSpec((comps, side_size), lambda i: (0, i))
    first = state is None
    in_specs = [
        small,
        small,
        small,
        pl.BlockSpec(pattern.shape, lambda i: (0, 0)),
        pl.BlockSpec(centers.shape, lambda i: (0, 0)),
        pl.BlockSpec((volumes, size), lambda i: (0, i)),
    ]
    args = [traces, left, right, pattern, centers, observed]
    if not first:
        in_specs += [foot_spec, side_spec]
        args += list(state)
    if final:
        out_specs = [foot_spec]
        out_shape = [jax.ShapeDtypeStruct((comps, flat), bf16)]
        scratch = []
    else:
        out_specs = [foot_spec, side_spec, small]
        out_shape = [
            jax.ShapeDtypeStruct((comps, flat), f32),
            jax.ShapeDtypeStruct((comps, blocks * side_size), f32),
            jax.ShapeDtypeStruct((comps, volumes), f32),
        ]
        scratch = [
            pltpu.VMEM((per_block * comps, per_block * volumes), f32),
            pltpu.VMEM((per_block * comps, LANES), f32),
        ]
    tall, flat_tall = per_block * comps, per_block * volumes
    scratch = [
        pltpu.VMEM((flat_tall, tall), bf16),
        pltpu.VMEM((tall, flat_tall), bf16),
        pltpu.VMEM((flat_tall, 2 * tall), bf16),
        pltpu.VMEM((2 * tall, flat_tall), bf16),
        pltpu.VMEM((tall, LANES), f32),
        pltpu.VMEM((2 * tall, LANES), f32),
    ] + scratch
    return pl.pallas_call(
        functools.partial(sweep_kernel, rows_patch, cols, first, final),
        grid=(blocks,),
        in_specs=in_specs,
        out_specs=out_specs,
        out_shape=out_shape,
        scratch_shapes=scratch,
        compiler_params=pltpu.CompilerParams(vmem_limit_bytes=VMEM_LIMIT),
        name="sweep",
    )(*args)


def exchange_kernel(count, traces_ref, left_ref, right_ref, landed, send_sem, recv_sem):
    me = lax.axis_index("narrow")
    right = lax.rem(me + 1, count)
    left = lax.rem(me + count - 1, count)
    barrier = pltpu.get_barrier_semaphore()
    for other in (left, right):
        pl.semaphore_signal(
            barrier, inc=1, device_id={"narrow": other}, device_id_type=pl.DeviceIdType.MESH
        )
    pl.semaphore_wait(barrier, 2)
    copies = []
    for k, other in enumerate((right, left)):
        copy = pltpu.make_async_remote_copy(
            src_ref=traces_ref,
            dst_ref=landed.at[k],
            send_sem=send_sem.at[k],
            recv_sem=recv_sem.at[k],
            device_id={"narrow": other},
            device_id_type=pl.DeviceIdType.MESH,
        )
        copy.start()
        copies.append(copy)
    for copy in copies:
        copy.wait()
    left_ref[...] = landed[0]
    right_ref[...] = landed[1]


def exchange(traces):
    shape = jax.ShapeDtypeStruct(traces.shape, f32)
    vmem = pl.BlockSpec(memory_space=pltpu.VMEM)
    return pl.pallas_call(
        functools.partial(exchange_kernel, lax.axis_size("narrow")),
        in_specs=[vmem],
        out_specs=[vmem, vmem],
        out_shape=[shape, shape],
        scratch_shapes=[
            pltpu.VMEM((2,) + traces.shape, f32),
            pltpu.SemaphoreType.DMA((2,)),
            pltpu.SemaphoreType.DMA((2,)),
        ],
        compiler_params=pltpu.CompilerParams(collective_id=0, has_side_effects=True),
        name="exchange",
    )(traces)


def from_neighbours(value, axis):
    count = lax.axis_size(axis)
    left = lax.ppermute(value, axis, [(i, i + 1) for i in range(count - 1)])
    right = lax.ppermute(value, axis, [(i + 1, i) for i in range(count - 1)])
    return left, right


def shards(recording, offsets, center_rows, center_cols, decays):
    frames_dev, height, cols = recording.shape
    wide = lax.axis_size("wide")
    narrow = lax.axis_size("narrow")
    rows_patch = height // wide
    ext_width = cols + EDGE
    comps = center_rows.shape[-1]

    head, tail = pack_edges(recording)
    ring = [(i, (i + 1) % narrow) for i in range(narrow)]
    tail = lax.ppermute(tail, "narrow", ring)
    head = lax.ppermute(head, "narrow", [(b, a) for a, b in ring])
    shifts = lax.dynamic_slice_in_dim(offsets, lax.axis_index("wide") * frames_dev, frames_dev, 1)
    chunks = CHUNKS if rows_patch % (CHUNKS * ROWS) == 0 else 1
    received = [
        lax.all_to_all(part, "wide", split_axis=0, concat_axis=0, tiled=True)
        for part in register(shifts, recording, head, tail, wide, chunks)
    ]

    place = np.arange(GROUP * ext_width)
    row = place // ext_width
    col = place % ext_width - MARGIN
    global_col = lax.axis_index("narrow") * cols + jnp.asarray(col, jnp.int32)
    inside = ((global_col >= 0) & (global_col < cols * narrow)).astype(f32)
    has_left = (lax.axis_index("narrow") > 0).astype(f32)
    has_right = (lax.axis_index("narrow") < narrow - 1).astype(f32)
    is_left = jnp.asarray(col < MARGIN, f32) * inside * has_left
    is_right = jnp.asarray(col >= cols - MARGIN, f32) * inside * has_right
    zero = jnp.zeros_like(inside)
    pattern = jnp.stack(
        [jnp.asarray(row, f32), jnp.asarray(col, f32), inside, is_left, is_right, zero, zero, zero]
    )
    centers = jnp.stack([center_rows[0, 0], center_cols[0, 0]], axis=1).astype(f32)
    left, right = from_neighbours(centers, "narrow")
    centers = jnp.concatenate(
        [centers, left, right, jnp.zeros((comps, LANES - 6), f32)], axis=1
    )

    earlier = None
    for chunk in range(chunks):
        earlier = observe(received[chunk], pattern, centers, earlier, rows_patch, chunk, chunks)
    observed, traces = earlier[:2]
    state = None
    for turn in range(ITERS):
        left, right = exchange(traces)
        final = turn == ITERS - 1
        out = sweep(
            traces, left, right, pattern, centers, observed, state, rows_patch, cols, final
        )
        if final:
            footprints = out[0]
        else:
            state, traces = out[:2], out[2]
    previous = jnp.concatenate([jnp.zeros((comps, 1), f32), traces[:, :-1]], axis=1)
    spikes = jnp.maximum(0.0, traces - decays[0, 0][:, None] * previous)
    return (
        footprints.reshape(1, 1, comps, -1),
        traces.reshape(1, 1, comps, VOLUMES),
        spikes.reshape(1, 1, comps, VOLUMES),
    )


def solution(mesh):
    in_specs = (
        P(("parts", "wide"), None, "narrow"),
        P(None, "parts"),
        P(("parts", "wide"), "narrow", None),
        P(("parts", "wide"), "narrow", None),
        P(("parts", "wide"), "narrow", None),
    )
    out_specs = (
        P(("parts", "wide"), "narrow", None, None),
        P(("parts", "wide"), "narrow", None, None),
        P(("parts", "wide"), "narrow", None, None),
    )
    return jax.shard_map(shards, mesh=mesh, in_specs=in_specs, out_specs=out_specs, check_vma=False)
```
